512 devices in a mesh: dp: 16 (over z_lo, x, core), tensor: 32 (over z_hi, y).
Axes of the slice: x: 4, y: 8, z: 8 (z_hi: 4, z_lo: 2; z = z_hi * 2 + z_lo), core: 2. Of those that a mesh axis runs over, the one named last changes fastest.
Arguments:
- attn_out: bfloat16 [4096, 8192], P('dp', 'tensor'), may hold values from -6 to 6
- teacher: bfloat16 [4096, 8192], P(('dp', 'tensor')), may hold values from -6 to 6
- int_codes: bfloat16 [8192, 8192], P(None, 'tensor'), may hold values from 0 to 15, as said below
- scales: float32 [64, 8192], P(None, 'tensor'), may hold values from 0.001 to 0.004
- offsets: float32 [64, 8192], P(None, 'tensor'), may hold values from 0.005 to 0.025
- lengths: int32 [32], replicated, may hold values from 1 to 128, 3072 in all
- shard_map: int32 [32], replicated, may hold values from 0 to 31, each once
Outputs:
- grad_scale: float32 [64, 8192], P(None, 'tensor')
- grad_offset: float32 [64, 8192], P(None, 'tensor')
The draws below stay inside these ranges and needn't reach their ends.
Inputs may be any that keep to these rules, and one draw needn't show every extreme that they name: `int_codes`: whole numbers. `lengths`: at least one sequence is full; they sum to 3072. `shard_map`: each block number once.
All inputs are finite; a program needn't handle non-finite values.
Results may differ from the reference program's by a relative error of at most 0.0023.
Values may be sent and summed in bfloat16 or wider, within the bound.
A program may use at most 128 MiB of HBM per device.

```python
import math
import jax
import jax.numpy as jnp
import numpy as np
from jax import lax

D = 8192
SEQ = 128
GROUPS = 64
SHARDS = 32
ROWS = 32
TOKENS = 4096
BLOCK = 8
N_DP = 16


def draw_int_codes(key, part):
    key = jax.random.fold_in(key, 11)
    return jax.random.randint(key, (D, D), 0, 16).astype(jnp.bfloat16)


def shard_levels(rng, shape, pieces, least, top_value):
    def one(axis_at, shards_of):
        heights = jax.random.uniform(jax.random.fold_in(jax.random.fold_in(rng, 6), axis_at), (shards_of,), jnp.float32, least / len(pieces), top_value / len(pieces))
        return jnp.repeat(jnp.exp(heights), shape[axis_at] // shards_of).reshape((-1,) + (1,) * (len(shape) - axis_at - 1))

    level = one(*pieces[0])
    for cut in pieces[1:]:
        level = level * one(*cut)
    return level


def profile(number_of, total, most, skew):
    weights = [(1 << 20) // math.isqrt(rank ** skew) + 1 for rank in range(2, number_of + 1)]
    spare, counts = total - most - (number_of - 1), [1] * (number_of - 1)
    while spare > 0:
        candidates = [i for i in range(number_of - 1) if counts[i] < most]
        pool, budget = sum([weights[i] for i in candidates]), spare
        for i in candidates:
            addition = min(most - counts[i], max(1, budget * weights[i] // pool), spare)
            counts[i] = counts[i] + addition
            spare = spare - addition
    return np.array([most] + counts)


def uneven(rng, count, total, reach, skew):
    if count == 2:
        one = jax.random.randint(rng, (), max(1, total - reach), min(reach, total - 1) + 1)
        return jnp.stack([one, total - one])
    sizes = jnp.asarray(profile(count, total, reach, skew), jnp.int32)
    pairs = (count - 1) // 2
    giver, receiver = sizes[1:1 + 2 * pairs:2], sizes[2:2 + 2 * pairs:2]
    room = jnp.minimum(giver - 1, reach - receiver)
    passed = jax.random.randint(jax.random.fold_in(rng, 1), (pairs,), 0, 1 << 20) % (room + 1)
    sizes = sizes.at[1:1 + 2 * pairs:2].set(giver - passed).at[2:2 + 2 * pairs:2].set(receiver + passed)
    return sizes[jax.random.permutation(jax.random.fold_in(rng, 2), count)]


def normal_values(own_key, dims, spread, most, split=(), kind=jnp.bfloat16):
    array = jax.random.normal(own_key, dims, jnp.float32) * spread
    if len(split) > 0:
        array = shard_levels(own_key, dims, split, -0.22, 0.18) * array
    return jnp.clip(array, min=-most, max=most).astype(kind)


def setup_inputs(seed: int = 0) -> dict:
    arg_keys = jax.random.split(jax.random.key(seed), 8)
    return {
        "attn_out": normal_values(arg_keys[0], (TOKENS, D), 1.0, 6.0, ((0, 16), (1, 32))),
        "teacher": normal_values(arg_keys[1], (TOKENS, D), 1.0, 6.0, ((0, 512),)),
        "int_codes": draw_int_codes(jax.random.fold_in(arg_keys[7], 71), 0),
        "scales": jnp.clip(jnp.exp(math.log(0.004) - 1.3862944 * jax.random.uniform(arg_keys[3], (GROUPS, D), jnp.float32) ** shard_levels(arg_keys[3], (GROUPS, D), ((1, 32),), -0.2, 0.2)), 0.001, 0.004),
        "offsets": jnp.clip(0.005 + 0.02 * jax.random.uniform(arg_keys[4], (GROUPS, D), jnp.float32) ** shard_levels(arg_keys[4], (GROUPS, D), ((1, 32),), -0.2, 0.2), 0.005, 0.025),
        "lengths": uneven(arg_keys[5], ROWS, ROWS * SEQ * 3 // 4, SEQ, 1).astype(jnp.int32),
        "shard_map": jax.random.permutation(arg_keys[6], SHARDS).astype(jnp.int32),
    }


def dequantize(int_codes, scales, offsets):
    group_count = scales.shape[0]
    in_rows = int_codes.shape[0]
    shaped = int_codes.astype(jnp.float32).reshape(group_count, in_rows // group_count, -1)
    return (shaped * scales[:, None, :] - offsets[:, None, :]).reshape(in_rows, -1).astype(jnp.bfloat16)


def inverse_of(shard_map):
    indices = jnp.arange(shard_map.shape[0], dtype=jnp.int32)
    hits = (shard_map[:, None] == indices[None, :]).astype(jnp.int32)
    return jnp.sum(indices[:, None] * hits, axis=0).astype(jnp.int32)


def live_rows(seq_lengths):
    positions = jnp.arange(SEQ, dtype=jnp.int32)
    return (positions[None, :] < seq_lengths[:, None]).astype(jnp.float32).reshape(-1)


def reduce_groups(weight_grad, int_codes, group_count):
    shaped = weight_grad.reshape(group_count, -1, weight_grad.shape[1])
    codes_f = int_codes.astype(jnp.float32).reshape(shaped.shape)
    return jnp.sum(shaped * codes_f, axis=1), -jnp.sum(shaped, axis=1)


def reference(attn_out, teacher, int_codes, scales, offsets, lengths, shard_map):
    weight = dequantize(int_codes, scales, offsets)
    student = jnp.dot(attn_out, weight, preferred_element_type=jnp.float32)
    inverse = inverse_of(shard_map)
    blocks = teacher.reshape(N_DP, SHARDS, BLOCK, D)
    target = jnp.take(blocks, inverse, axis=1).reshape(TOKENS, D)
    live_mask = live_rows(lengths)
    live_total = jnp.sum(lengths).astype(jnp.float32)
    cotangent = (2.0 * (student - target.astype(jnp.float32)) * live_mask[:, None] / live_total).astype(jnp.bfloat16)
    weight_grad = lax.dot_general(attn_out, cotangent, (((0,), (0,)), ((), ())), preferred_element_type=jnp.float32)
    grad_scale, grad_offset = reduce_groups(weight_grad, int_codes, GROUPS)
    return (grad_scale, grad_offset)
```

```python
import functools

import jax
import jax.numpy as jnp
from jax import lax
from jax.experimental import pallas as pl
from jax.experimental.pallas import tpu as pltpu
from jax.sharding import PartitionSpec as P

SEQ = 128
R1 = 160
R2 = 96
H1, H2 = R1 // 2, R2 // 2
T = R1 + R2
NY, NZ = 8, 4
NT = NY * NZ
NDP = 16
C = 256
GROUPS = 64
F32, BF16 = jnp.float32, jnp.bfloat16
MESH = pl.DeviceIdType.MESH


def kernel(
    lengths, shard_map, attn, teacher, codes_hbm, scales, offsets, out,
    a1, a2, codes, weight, parts, acc, rowsum, t_land, target, grads, rs_land,
    loc_sem, y1s, y1r, z1s, z1r, y2s, y2r, z2s, z2r, ts, tr, rss, rsr, ags, agr,
):
    dp = lax.axis_index("dp")
    me = lax.axis_index("tensor")
    zh, y = me // NY, me % NY

    def slot_of(z, yy):
        return z * NY + yy

    def dev(z, yy):
        return (dp, slot_of(z, yy))

    y_nb = (dev(zh, (y + 1) % NY), dev(zh, (y + NY - 1) % NY))
    z_nb = (dev((zh + 1) % NZ, y), dev((zh + NZ - 1) % NZ, y))

    def remote(src, dst, ssem, rsem, to):
        return pltpu.make_async_remote_copy(
            src_ref=src, dst_ref=dst, send_sem=ssem, recv_sem=rsem,
            device_id=to, device_id_type=MESH,
        )

    loc = [
        pltpu.make_async_copy(attn.at[pl.ds(0, R1)], a1.at[me], loc_sem.at[0]),
        pltpu.make_async_copy(attn.at[pl.ds(R1, R2)], a2.at[me], loc_sem.at[1]),
        pltpu.make_async_copy(codes_hbm, codes, loc_sem.at[2]),
        pltpu.make_async_copy(
            teacher.at[:, pl.ds(pl.multiple_of(me * C, C), C)], t_land.at[me], loc_sem.at[3]
        ),
    ]
    for c in loc:
        c.start()

    barrier = pltpu.get_barrier_semaphore()

    @pl.loop(1, NT)
    def _(i):
        pl.semaphore_signal(barrier, 1, device_id=(dp, (me + i) % NT), device_id_type=MESH)

    @pl.loop(1, NDP)
    def _(i):
        pl.semaphore_signal(barrier, 1, device_id=((dp + i) % NDP, me), device_id_type=MESH)

    pl.semaphore_wait(barrier, NT - 1 + NDP - 1)
    loc[0].wait()
    loc[1].wait()

    def z1_full(d):
        src = slot_of(zh, y)
        return remote(a1.at[src], a1.at[src], z1s.at[d], z1r.at[d], z_nb[d])

    def z1_half(d):
        src = slot_of((zh + (NZ - 1 if d == 0 else 1)) % NZ, y)
        ref = a1.at[src, pl.ds(d * H1, H1)]
        return remote(ref, ref, z1s.at[2 + d], z1r.at[2 + d], z_nb[d])

    def y1_slot(s, k, d):
        off = k + k // 2 - 2 * (k // 3)
        yy = (y + NY - s) % NY if d == 0 else (y + s) % NY
        return slot_of((zh + off) % NZ, yy)

    def y1_full(s, k, d):
        ref = a1.at[y1_slot(s, k, d)]
        return remote(ref, ref, y1s.at[s, k, d], y1r.at[s, k, d], y_nb[d])

    def y1_half(k, d):
        ref = a1.at[y1_slot(3, k, d), pl.ds(d * H1, H1)]
        return remote(ref, ref, y1s.at[3, k, d], y1r.at[3, k, d], y_nb[d])

    def y2_slot(s, d):
        return slot_of(zh, (y + NY - s) % NY if d == 0 else (y + s) % NY)

    def y2_full(s, d):
        ref = a2.at[y2_slot(s, d)]
        return remote(ref, ref, y2s.at[s, d], y2r.at[s, d], y_nb[d])

    def y2_half(d):
        ref = a2.at[y2_slot(3, d), pl.ds(d * H2, H2)]
        return remote(ref, ref, y2s.at[3, d], y2r.at[3, d], y_nb[d])

    def y_of(m):
        dist = (m + 1) // 2
        odd = m % 2
        return (y + NY + dist * (1 - 2 * odd)) % NY

    def z2_full(m, d):
        ref = a2.at[slot_of(zh, y_of(m))]
        return remote(ref, ref, z2s.at[m, d], z2r.at[m, d], z_nb[d])

    def z2_half(m, d):
        src = slot_of((zh + (NZ - 1 if d == 0 else 1)) % NZ, y_of(m))
        ref = a2.at[src, pl.ds(d * H2, H2)]
        return remote(ref, ref, z2s.at[m, 2 + d], z2r.at[m, 2 + d], z_nb[d])

    for d in range(2):
        z1_full(d).start()
        y2_full(0, d).start()
        y1_full(0, 0, d).start()
        z2_full(0, d).start()

    def t_copy(i):
        to = (me + i) % NT
        return remote(
            teacher.at[:, pl.ds(pl.multiple_of(to * C, C), C)], t_land.at[me],
            ts.at[i], tr.at[i], (dp, to),
        )

    @pl.loop(1, NT)
    def _(i):
        t_copy(i).start()

    loc[2].wait()
    acc[...] = jnp.zeros_like(acc)
    rowsum[...] = jnp.zeros_like(rowsum)

    @pl.loop(0, GROUPS)
    def _(g):
        rows = pl.ds(pl.multiple_of(g * 128, 128), 128)
        weight[rows, :] = (
            codes[rows, :].astype(F32) * scales[pl.ds(g, 1), :] - offsets[pl.ds(g, 1), :]
        ).astype(BF16)

    group_iota = lax.broadcasted_iota(jnp.int32, (GROUPS, C), 0)
    feat_half = lax.broadcasted_iota(jnp.int32, (GROUPS, C), 1) // 128

    def use(a, slot, first, rows):
        at = pl.ds(first, rows)
        k0 = pl.ds(pl.multiple_of(slot * C, C), C)
        ka = pl.ds(pl.multiple_of(slot * C, C), 128)
        kb = pl.ds(pl.multiple_of(slot * C + 128, 128), 128)
        acc[at, :] += jnp.dot(a, weight[k0, :], preferred_element_type=F32)
        parts[2 * slot, at, :] = jnp.dot(a[:, :128], codes[ka, :], preferred_element_type=F32)
        parts[2 * slot + 1, at, :] = jnp.dot(a[:, 128:], codes[kb, :], preferred_element_type=F32)
        pick = (group_iota == 2 * slot + feat_half).astype(BF16)
        pad = jnp.zeros((T - rows, C), BF16)
        whole = jnp.concatenate([a, pad] if first == 0 else [pad, a], axis=0)
        rowsum[...] += lax.dot_general(
            pick, whole, (((1,), (1,)), ((), ())), preferred_element_type=F32
        )

    def use1(slot):
        use(a1[slot], slot, 0, R1)

    def use2(slot):
        use(a2[slot], slot, R1, R2)

    def make_target():
        loc[3].wait()

        @pl.loop(1, NT)
        def _(i):
            t_copy(i).wait_recv()

        lane = lax.broadcasted_iota(jnp.int32, (8, T), 1)
        where_to = jnp.zeros((8, T), jnp.int32)
        for j in range(NT):
            where_to = jnp.where(lane // 8 == j, shard_map[j] * 8 + lane % 8, where_to)
        row = lax.broadcasted_iota(jnp.int32, (T, T), 0)
        perm = (row == where_to[:1, :]).astype(F32).astype(BF16)
        arrived = t_land[...].astype(F32).reshape(T, C).astype(BF16)
        target[...] = jnp.dot(perm, arrived, preferred_element_type=F32)

    LAG1, LAG2 = 6, 12

    @pl.loop(0, 20)
    def _(n):
        s, k = n // 4, n % 4

        @pl.when(s == 0)
        def _():
            @pl.when(k == 1)
            def _():
                z1_full(1).wait_recv()
                z1_half(1).start()

            @pl.when(k == 2)
            def _():
                z1_full(0).wait_recv()
                z1_half(0).start()

            @pl.when(k == 3)
            def _():
                z1_half(0).wait_recv()
                z1_half(1).wait_recv()

            @pl.when(k > 0)
            def _():
                y1_full(0, k, 0).start()
                y1_full(0, k, 1).start()

        for sv in (1, 2):
            @pl.when(s == sv)
            def _():
                for d in range(2):
                    y1_full(sv - 1, k, d).wait_recv()
                    y1_full(sv, k, d).start()

        @pl.when(s == 3)
        def _():
            for d in range(2):
                y1_full(2, k, d).wait_recv()
                y1_half(k, d).start()

        @pl.when(s == 4)
        def _():
            for d in range(2):
                y1_half(k, d).wait_recv()

        m = n

        @pl.when((m >= 1) & (m <= 7))
        def _():
            dist = (m + 1) // 2
            for d in range(2):
                @pl.when((m % 2 == 1 - d) & (m < 7))
                def _():
                    y2_full(dist - 1, d).wait_recv()

                    @pl.when(dist < 3)
                    def _():
                        y2_full(dist, d).start()

                    @pl.when(dist == 3)
                    def _():
                        y2_half(d).start()

            @pl.when(m == 7)
            def _():
                y2_half(0).wait_recv()
                y2_half(1).wait_recv()

            z2_full(m, 0).start()
            z2_full(m, 1).start()

        m1 = n - LAG1

        @pl.when((m1 >= 0) & (m1 < 8))
        def _():
            for d in range(2):
                z2_full(m1, d).wait_recv()
                z2_half(m1, d).start()

        m2 = n - LAG2

        @pl.when(m2 >= 0)
        def _():
            for d in range(2):
                z2_half(m2, d).wait_recv()

        use1(y1_slot(s, k, 0))

        @pl.when((s > 0) & (s < 4))
        def _():
            use1(y1_slot(s, k, 1))

        count = (m < 8).astype(jnp.int32) + 2 * ((m1 >= 0) & (m1 < 8)).astype(jnp.int32)

        @pl.when(m < 8)
        def _():
            use2(slot_of(zh, y_of(m)))

        @pl.when((m1 >= 0) & (m1 < 8))
        def _():
            @pl.loop(0, 2)
            def _(d):
                use2(slot_of((zh + 1 + 2 * d) % NZ, y_of(m1)))

        @pl.when(m2 >= 0)
        def _():
            use2(slot_of((zh + 2) % NZ, y_of(m2)))

        @pl.when(n == 14)
        def _():
            make_target()

    total = lengths[0]
    for i in range(1, 32):
        total = total + lengths[i]
    token = lax.broadcasted_iota(jnp.int32, (T, C), 0)
    limit = jnp.where(token < SEQ, lengths[2 * dp], lengths[2 * dp + 1] + SEQ)
    live = (token < limit).astype(F32)
    cot16 = (2.0 * (acc[...] - target[...]) * live / total.astype(F32)).astype(BF16)
    acc[...] = cot16.astype(F32)

    rs = rowsum[...]
    hi = rs.astype(BF16)
    rest = rs - hi.astype(F32)
    mid = rest.astype(BF16)
    low = (rest - mid.astype(F32)).astype(BF16)
    offs = jnp.dot(hi, cot16, preferred_element_type=F32)
    offs += jnp.dot(mid, cot16, preferred_element_type=F32)
    offs += jnp.dot(low, cot16, preferred_element_type=F32)
    grads[pl.ds(8, 8)] = -offs.reshape(8, 8, C)

    def rs_copy(c):
        return remote(grads.at[c], rs_land.at[dp], rss.at[c], rsr.at[dp], (c, me))

    def rs_wait(src):
        return remote(grads.at[src], rs_land.at[src], rss.at[src], rsr.at[src], (src, me))

    @pl.loop(8, 16)
    def _(c):
        @pl.when(c != dp)
        def _():
            rs_copy(c).start()

    @pl.loop(0, 8)
    def _(c):
        for q in range(8):
            prod = parts[c * 8 + q] * acc[...]
            grads[c, pl.ds(q, 1), :] = jnp.sum(prod, axis=0, keepdims=True)

        @pl.when(c != dp)
        def _():
            rs_copy(c).start()

    rs_land[dp] = grads[dp]

    @pl.loop(0, NDP)
    def _(c):
        @pl.when(c != dp)
        def _():
            rs_wait(c).wait_recv()

    out[dp] = jnp.sum(rs_land[...], axis=0)

    def ag_copy(c):
        return remote(out.at[dp], out.at[dp], ags.at[c], agr.at[dp], (c, me))

    def ag_wait(src):
        return remote(out.at[src], out.at[src], ags.at[src], agr.at[src], (src, me))

    @pl.loop(0, NDP)
    def _(c):
        @pl.when(c != dp)
        def _():
            ag_copy(c).start()

    for d in range(2):
        z1_full(d).wait_send()
        z1_half(d).wait_send()
        y2_half(d).wait_send()

        @pl.loop(0, 4)
        def _(k):
            for s in range(3):
                y1_full(s, k, d).wait_send()
            y1_half(k, d).wait_send()

        for s in range(3):
            y2_full(s, d).wait_send()

        @pl.loop(0, 8)
        def _(m):
            z2_full(m, d).wait_send()
            z2_half(m, d).wait_send()

    @pl.loop(1, NT)
    def _(i):
        t_copy(i).wait_send()

    @pl.loop(0, NDP)
    def _(c):
        @pl.when(c != dp)
        def _():
            rs_copy(c).wait_send()
            ag_wait(c).wait_recv()
            ag_copy(c).wait_send()


def per_device(attn_out, teacher, int_codes, scales, offsets, lengths, shard_map):
    dma = pltpu.SemaphoreType.DMA
    vmem = pl.BlockSpec(memory_space=pltpu.VMEM)
    smem = pl.BlockSpec(memory_space=pltpu.SMEM)
    hbm = pl.BlockSpec(memory_space=pl.ANY)
    out = pl.pallas_call(
        kernel,
        out_shape=jax.ShapeDtypeStruct((NDP, 8, C), F32),
        in_specs=[smem, smem, hbm, hbm, hbm, vmem, vmem],
        out_specs=vmem,
        scratch_shapes=[
            pltpu.VMEM((NT, R1, C), BF16),
            pltpu.VMEM((NT, R2, C), BF16),
            pltpu.VMEM((8192, C), BF16),
            pltpu.VMEM((8192, C), BF16),
            pltpu.VMEM((GROUPS, T, C), F32),
            pltpu.VMEM((T, C), F32),
            pltpu.VMEM((GROUPS, T), F32),
            pltpu.VMEM((NT, 8, C), BF16),
            pltpu.VMEM((T, C), F32),
            pltpu.VMEM((NDP, 8, C), F32),
            pltpu.VMEM((NDP, 8, C), F32),
            dma((4,)),
            dma((4, 4, 2)), dma((4, 4, 2)),
            dma((4,)), dma((4,)),
            dma((4, 2)), dma((4, 2)),
            dma((8, 4)), dma((8, 4)),
            dma((NT,)), dma((NT,)),
            dma((NDP,)), dma((NDP,)),
            dma((NDP,)), dma((NDP,)),
        ],
        compiler_params=pltpu.CompilerParams(
            collective_id=0, has_side_effects=True, vmem_limit_bytes=48 << 20
        ),
        cost_estimate=pl.CostEstimate(
            flops=3 * 2 * T * 8192 * C, bytes_accessed=6 << 20, transcendentals=0
        ),
    )(lengths, shard_map, attn_out, teacher, int_codes, scales, offsets)
    flat = out.reshape(128, C)
    return flat[:64], flat[64:]


def solution(mesh):
    in_specs = (
        P("dp", "tensor"),
        P(("dp", "tensor"), None),
        P(None, "tensor"),
        P(None, "tensor"),
        P(None, "tensor"),
        P(),
        P(),
    )
    out_specs = (P(None, "tensor"), P(None, "tensor"))
    return jax.shard_map(
        per_device, mesh=mesh, in_specs=in_specs, out_specs=out_specs, check_vma=False
    )
```

```python
import functools

import jax
import jax.numpy as jnp
from jax import lax
from jax.experimental import pallas as pl
from jax.experimental.pallas import tpu as pltpu
from jax.sharding import PartitionSpec as P

SEQ = 128
R1 = 160
R2 = 96
H1, H2 = R1 // 2, R2 // 2
T = R1 + R2
NY, NZ = 8, 4
NT = NY * NZ
NDP = 16
C = 256
GROUPS = 64
F32, BF16 = jnp.float32, jnp.bfloat16
MESH = pl.DeviceIdType.MESH
PART1 = [
    (0, 0), (1, 0), (0, 1), (0, 2), (2, 0), (1, 1), (1, 2), (0, 3), (3, 0), (2, 1),
    (2, 2), (1, 3), (3, 1), (3, 2), (4, 0), (2, 3), (4, 1), (4, 2), (3, 3), (4, 3),
]
PART2_Y = [0, 1, 2, -1, 3, 4, -1, 5, 6, -1, 7, -1, -1, -1, -1, -1, -1, -1, -1, -1]
PART2_Z = [-1, -1, -1, -1, 0, -1, 1, -1, 2, -1, 3, -1, 4, -1, 5, -1, 6, 7, -1, -1]
PART2_ZZ = [-1, -1, -1, -1, -1, -1, -1, -1, -1, 0, -1, 1, -1, 2, -1, 3, 4, 5, 6, 7]


def kernel(
    lengths_hbm, shard_map_hbm, attn, teacher, codes_hbm, scales_hbm, offsets_hbm, out,
    lengths, shard_map, scales, offsets, a1, a2, codes, weight, parts, acc, rowsum, tz_land, t_land, target, grads, rs_land,
    loc_sem, a1s, a2s, y1r, z1r, y2r, y2hr, z2r, z2hr, tzs, tzr, tys, tyr, hello, rss, rsr, ags, agr,
):
    dp = lax.axis_index("dp")
    me = lax.axis_index("tensor")
    zh, y = me // NY, me % NY

    def slot_of(z, yy):
        return z * NY + yy

    def dev(z, yy):
        return (dp, slot_of(z, yy))

    y_nb = (dev(zh, (y + 1) % NY), dev(zh, (y + NY - 1) % NY))
    z_nb = (dev((zh + 1) % NZ, y), dev((zh + NZ - 1) % NZ, y))

    def remote(src, dst, ssem, rsem, to):
        return pltpu.make_async_remote_copy(
            src_ref=src, dst_ref=dst, send_sem=ssem, recv_sem=rsem,
            device_id=to, device_id_type=MESH,
        )

    def wait_all(ref, sem):
        pltpu.make_async_copy(ref, ref, sem).wait()

    zl, x, core = dp // 8, dp // 2 % 4, dp % 2

    def peer(zl_, x_, core_):
        return (zl_ * 8 + x_ * 2 + core_, me)

    dp_nb = (
        peer(zl, x, 1 - core), peer(1 - zl, x, core),
        peer(zl, (x + 1) % 4, core), peer(zl, (x + 3) % 4, core),
    )
    barrier = pltpu.get_barrier_semaphore()
    for to in y_nb + z_nb + dp_nb:
        pl.semaphore_signal(barrier, 1, device_id=to, device_id_type=MESH)

    def say_hello(r):
        for to in dp_nb:
            pl.semaphore_signal(hello.at[r], 1, device_id=to, device_id_type=MESH)

    def hear_hello(r):
        pl.semaphore_wait(hello.at[r], 4)

    loc = [
        pltpu.make_async_copy(attn.at[pl.ds(0, R1)], a1.at[me], loc_sem.at[0]),
        pltpu.make_async_copy(attn.at[pl.ds(R1, R2)], a2.at[me], loc_sem.at[1]),
        pltpu.make_async_copy(codes_hbm, codes, loc_sem.at[2]),
        pltpu.make_async_copy(scales_hbm, scales, loc_sem.at[3]),
        pltpu.make_async_copy(offsets_hbm, offsets, loc_sem.at[4]),
        pltpu.make_async_copy(lengths_hbm, lengths, loc_sem.at[5]),
        pltpu.make_async_copy(shard_map_hbm, shard_map, loc_sem.at[6]),
        pltpu.make_async_copy(
            teacher.at[:, pl.ds(pl.multiple_of(zh * NY * C, C), NY * C)], tz_land.at[zh], loc_sem.at[7]
        ),
    ]
    for c in loc:
        c.start()

    pl.semaphore_wait(barrier, 8)
    say_hello(0)
    loc[0].wait()
    loc[1].wait()

    def z1_full(d):
        src = slot_of(zh, y)
        return remote(a1.at[src], a1.at[src], a1s, z1r.at[d], z_nb[d])

    def z1_half(d):
        src = slot_of((zh + (NZ - 1 if d == 0 else 1)) % NZ, y)
        ref = a1.at[src, pl.ds(d * H1, H1)]
        return remote(ref, ref, a1s, z1r.at[2], z_nb[d])

    def y1_slot(s, k, d):
        off = k + k // 2 - 2 * (k // 3)
        yy = (y + NY - s) % NY if d == 0 else (y + s) % NY
        return slot_of((zh + off) % NZ, yy)

    def y1_full(s, k, d):
        ref = a1.at[y1_slot(s, k, d)]
        return remote(ref, ref, a1s, y1r.at[s, k], y_nb[d])

    def y1_half(k, d):
        ref = a1.at[y1_slot(3, k, d), pl.ds(d * H1, H1)]
        return remote(ref, ref, a1s, y1r.at[3, k], y_nb[d])

    def y2_slot(s, d):
        return slot_of(zh, (y + NY - s) % NY if d == 0 else (y + s) % NY)

    def y2_full(s, d):
        ref = a2.at[y2_slot(s, d)]
        return remote(ref, ref, a2s, y2r.at[s, d], y_nb[d])

    def y2_half(d):
        ref = a2.at[y2_slot(3, d), pl.ds(d * H2, H2)]
        return remote(ref, ref, a2s, y2hr, y_nb[d])

    def y_of(m):
        dist = (m + 1) // 2
        odd = m % 2
        return (y + NY + dist * (1 - 2 * odd)) % NY

    def z2_full(m, d):
        ref = a2.at[slot_of(zh, y_of(m))]
        return remote(ref, ref, a2s, z2r.at[m], z_nb[d])

    def z2_half(m, d):
        src = slot_of((zh + (NZ - 1 if d == 0 else 1)) % NZ, y_of(m))
        ref = a2.at[src, pl.ds(d * H2, H2)]
        return remote(ref, ref, a2s, z2hr.at[m], z_nb[d])

    for d in range(2):
        z1_full(d).start()
        y2_full(0, d).start()
        y1_full(0, 0, d).start()
        z2_full(0, d).start()

    def tz_copy(i):
        zt = (zh + i) % NZ
        return remote(
            teacher.at[:, pl.ds(pl.multiple_of(zt * NY * C, C), NY * C)], tz_land.at[zh],
            tzs, tzr, dev(zt, y),
        )

    def ty_copy(i):
        yt = (y + i) % NY
        return remote(
            tz_land.at[:, :, pl.ds(pl.multiple_of(yt * C, C), C)], t_land.at[y],
            tys, tyr, dev(zh, yt),
        )

    tz_copy(1).start()
    tz_copy(3).start()

    for c in loc[2:7]:
        c.wait()
    acc[...] = jnp.zeros_like(acc)
    rowsum[...] = jnp.zeros_like(rowsum)

    @pl.loop(0, GROUPS)
    def _(g):
        rows = pl.ds(pl.multiple_of(g * 128, 128), 128)
        weight[rows, :] = (
            codes[rows, :].astype(F32) * scales[pl.ds(g, 1), :] - offsets[pl.ds(g, 1), :]
        ).astype(BF16)

    group_iota = lax.broadcasted_iota(jnp.int32, (GROUPS, C), 0)
    feat_half = lax.broadcasted_iota(jnp.int32, (GROUPS, C), 1) // 128

    def use(a, slot, first, rows):
        at = pl.ds(first, rows)
        k0 = pl.ds(pl.multiple_of(slot * C, C), C)
        ka = pl.ds(pl.multiple_of(slot * C, C), 128)
        kb = pl.ds(pl.multiple_of(slot * C + 128, 128), 128)
        acc[at, :] += jnp.dot(a, weight[k0, :], preferred_element_type=F32)
        parts[2 * slot, at, :] = jnp.dot(a[:, :128], codes[ka, :], preferred_element_type=F32)
        parts[2 * slot + 1, at, :] = jnp.dot(a[:, 128:], codes[kb, :], preferred_element_type=F32)
        pick = (group_iota == 2 * slot + feat_half).astype(BF16)
        pad = jnp.zeros((T - rows, C), BF16)
        whole = jnp.concatenate([a, pad] if first == 0 else [pad, a], axis=0)
        rowsum[...] += lax.dot_general(
            pick, whole, (((1,), (1,)), ((), ())), preferred_element_type=F32
        )

    def use1(slot):
        use(a1[slot], slot, 0, R1)

    def use2(slot):
        use(a2[slot], slot, R1, R2)

    def make_target():
        wait_all(t_land.at[pl.ds(0, NY - 1)], tyr)
        own_t.wait()

        lane = lax.broadcasted_iota(jnp.int32, (8, T), 1)
        where_to = jnp.zeros((8, T), jnp.int32)
        for j in range(NT):
            where_to = jnp.where(
                lane // 8 == j % NY * NZ + j // NY, shard_map[j] * 8 + lane % 8, where_to
            )
        row = lax.broadcasted_iota(jnp.int32, (T, T), 0)
        perm = (row == where_to[:1, :]).astype(F32).astype(BF16)
        arrived = t_land[...].astype(F32).reshape(T, C).astype(BF16)
        target[...] = jnp.dot(perm, arrived, preferred_element_type=F32)

    own_t = pltpu.make_async_copy(
        tz_land.at[:, :, pl.ds(pl.multiple_of(y * C, C), C)], t_land.at[y], loc_sem.at[8]
    )

    def entry(table, n):
        value = jnp.int32(table[0])
        for i, item in enumerate(table):
            value = jnp.where(n == i, item, value)
        return value

    @pl.loop(0, len(PART1))
    def _(n):
        s = entry([e[0] for e in PART1], n)
        k = entry([e[1] for e in PART1], n)
        m, m1, m2 = entry(PART2_Y, n), entry(PART2_Z, n), entry(PART2_ZZ, n)

        @pl.when(s == 0)
        def _():
            @pl.when(k == 1)
            def _():
                z1_full(1).wait_recv()
                z1_half(1).start()

            @pl.when(k == 2)
            def _():
                z1_full(0).wait_recv()
                z1_half(0).start()

            @pl.when(k == 3)
            def _():
                wait_all(a1.at[0], z1r.at[2])

            @pl.when(k > 0)
            def _():
                y1_full(0, k, 0).start()
                y1_full(0, k, 1).start()

        for sv in (1, 2):
            @pl.when(s == sv)
            def _():
                wait_all(a1.at[pl.ds(0, 2)], y1r.at[sv - 1, k])
                for d in range(2):
                    y1_full(sv, k, d).start()

        @pl.when(s == 3)
        def _():
            wait_all(a1.at[pl.ds(0, 2)], y1r.at[2, k])
            for d in range(2):
                y1_half(k, d).start()

        @pl.when(s == 4)
        def _():
            wait_all(a1.at[0], y1r.at[3, k])

        @pl.when(m >= 1)
        def _():
            dist = (m + 1) // 2
            for d in range(2):
                @pl.when((m % 2 == 1 - d) & (m < 7))
                def _():
                    y2_full(dist - 1, d).wait_recv()

                    @pl.when(dist < 3)
                    def _():
                        y2_full(dist, d).start()

                    @pl.when(dist == 3)
                    def _():
                        y2_half(d).start()

            @pl.when(m == 7)
            def _():
                wait_all(a2.at[0], y2hr)

            z2_full(m, 0).start()
            z2_full(m, 1).start()

        @pl.when(m1 >= 0)
        def _():
            wait_all(a2.at[pl.ds(0, 2)], z2r.at[m1])
            for d in range(2):
                z2_half(m1, d).start()

        @pl.when(m2 >= 0)
        def _():
            wait_all(a2.at[0], z2hr.at[m2])

        use1(y1_slot(s, k, 0))

        @pl.when((s > 0) & (s < 4))
        def _():
            use1(y1_slot(s, k, 1))

        @pl.when(m >= 0)
        def _():
            use2(slot_of(zh, y_of(m)))

        @pl.when(m1 >= 0)
        def _():
            @pl.loop(0, 2)
            def _(d):
                use2(slot_of((zh + 1 + 2 * d) % NZ, y_of(m1)))

        @pl.when(m2 >= 0)
        def _():
            use2(slot_of((zh + 2) % NZ, y_of(m2)))

        for r in range(3):
            @pl.when(n == 3 + 3 * r)
            def _():
                hear_hello(r)
                if r < 2:
                    say_hello(r + 1)

        @pl.when(n == 8)
        def _():
            tz_copy(2).start()

        @pl.when(n == 12)
        def _():
            loc[7].wait()
            wait_all(tz_land.at[pl.ds(0, NZ - 1)], tzr)
            own_t.start()

            @pl.loop(1, NY)
            def _(i):
                ty_copy(i).start()

        @pl.when(n == 17)
        def _():
            make_target()

    total = lengths[0]
    for i in range(1, 32):
        total = total + lengths[i]
    token = lax.broadcasted_iota(jnp.int32, (T, C), 0)
    limit = jnp.where(token < SEQ, lengths[2 * dp], lengths[2 * dp + 1] + SEQ)
    live = (token < limit).astype(F32)
    cot16 = (2.0 * (acc[...] - target[...]) * live / total.astype(F32)).astype(BF16)
    acc[...] = cot16.astype(F32)

    rs = rowsum[...]
    hi = rs.astype(BF16)
    rest = rs - hi.astype(F32)
    mid = rest.astype(BF16)
    low = (rest - mid.astype(F32)).astype(BF16)
    offs = jnp.dot(hi, cot16, preferred_element_type=F32)
    offs += jnp.dot(mid, cot16, preferred_element_type=F32)
    offs += jnp.dot(low, cot16, preferred_element_type=F32)
    grads[pl.ds(8, 8)] = -offs.reshape(8, 8, C)

    def rs_copy(c):
        return remote(grads.at[c], rs_land.at[dp], rss, rsr, (c, me))

    @pl.loop(8, 16)
    def _(c):
        @pl.when(c != dp)
        def _():
            rs_copy(c).start()

    @pl.loop(0, 8)
    def _(c):
        for q in range(8):
            prod = parts[c * 8 + q] * acc[...]
            grads[c, pl.ds(q, 1), :] = jnp.sum(prod, axis=0, keepdims=True)

        @pl.when(c != dp)
        def _():
            rs_copy(c).start()

    rs_land[dp] = grads[dp]

    wait_all(rs_land.at[pl.ds(0, NDP - 1)], rsr)

    out[dp] = jnp.sum(rs_land[...], axis=0)

    def ag_copy(c):
        return remote(out.at[dp], out.at[dp], ags, agr, (c, me))

    @pl.loop(0, NDP)
    def _(c):
        @pl.when(c != dp)
        def _():
            ag_copy(c).start()

    wait_all(a1.at[pl.ds(0, NT - 1)], a1s)
    wait_all(a2.at[pl.ds(0, NT - 1)], a2s)
    wait_all(tz_land.at[pl.ds(0, NZ - 1)], tzs)
    wait_all(t_land.at[pl.ds(0, NY - 1)], tys)
    wait_all(rs_land.at[pl.ds(0, NDP - 1)], rss)
    wait_all(out.at[pl.ds(0, NDP - 1)], agr)
    wait_all(out.at[pl.ds(0, NDP - 1)], ags)


def per_device(attn_out, teacher, int_codes, scales, offsets, lengths, shard_map):
    dma = pltpu.SemaphoreType.DMA
    vmem = pl.BlockSpec(memory_space=pltpu.VMEM)
    hbm = pl.BlockSpec(memory_space=pltpu.HBM)
    out = pl.pallas_call(
        kernel,
        out_shape=pltpu.VMEM((NDP, 8, C), F32),
        in_specs=[hbm] * 7,
        out_specs=vmem,
        scratch_shapes=[
            pltpu.SMEM((32,), jnp.int32),
            pltpu.SMEM((32,), jnp.int32),
            pltpu.VMEM((GROUPS, C), F32),
            pltpu.VMEM((GROUPS, C), F32),
            pltpu.VMEM((NT, R1, C), BF16),
            pltpu.VMEM((NT, R2, C), BF16),
            pltpu.VMEM((8192, C), BF16),
            pltpu.VMEM((8192, C), BF16),
            pltpu.VMEM((GROUPS, T, C), F32),
            pltpu.VMEM((T, C), F32),
            pltpu.VMEM((GROUPS, T), F32),
            pltpu.VMEM((NZ, 8, NY * C), BF16),
            pltpu.VMEM((NY, NZ, 8, C), BF16),
            pltpu.VMEM((T, C), F32),
            pltpu.VMEM((NDP, 8, C), F32),
            pltpu.VMEM((NDP, 8, C), F32),
            dma((9,)),
            dma(()), dma(()),
            dma((4, 4)), dma((3,)),
            dma((3, 2)), dma(()),
            dma((8,)), dma((8,)),
            dma(()), dma(()), dma(()), dma(()),
            pltpu.SemaphoreType.REGULAR((3,)),
            dma(()), dma(()), dma(()), dma(()),
        ],
        compiler_params=pltpu.CompilerParams(
            collective_id=0, has_side_effects=True, vmem_limit_bytes=63 << 20
        ),
        cost_estimate=pl.CostEstimate(
            flops=3 * 2 * T * 8192 * C, bytes_accessed=6 << 20, transcendentals=0
        ),
    )(lengths, shard_map, attn_out, teacher, int_codes, scales, offsets)
    flat = out.reshape(128, C)
    return flat[:64], flat[64:]


def solution(mesh):
    in_specs = (
        P("dp", "tensor"),
        P(("dp", "tensor"), None),
        P(None, "tensor"),
        P(None, "tensor"),
        P(None, "tensor"),
        P(),
        P(),
    )
    out_specs = (P(None, "tensor"), P(None, "tensor"))
    return jax.shard_map(
        per_device, mesh=mesh, in_specs=in_specs, out_specs=out_specs, check_vma=False
    )
```

```python
import jax
import jax.numpy as jnp
from jax import lax
from jax.experimental import pallas as pl
from jax.experimental.pallas import tpu as pltpu
from jax.sharding import PartitionSpec as P

SEQ = 128
T = 256
C = 256
NY, NZ = 8, 4
NT = NY * NZ
NDP = 16
GROUPS = 64
F32, BF16 = jnp.float32, jnp.bfloat16
MESH = pl.DeviceIdType.MESH
EVENTS = [
    (0, 0), (1, 0), (0, 1), (0, 2), (2, 0), (1, 1), (1, 2), (0, 3), (3, 0), (2, 1),
    (2, 2), (1, 3), (3, 1), (3, 2), (4, 0), (2, 3), (4, 1), (4, 2), (3, 3), (4, 3),
]
PIECE = [0, 1, 0, 2, 1, 3, 2, 4, 3, 5, 4, 6, 5, 7, 6, 7]
DIRECT = [1, 1, 0, 1, 0, 1, 0, 1, 0, 1, 0, 1, 0, 1, 0, 0]
LAG1, LAG2 = 4, 8
AHEAD = 3
HELLOS = 4


def entry(table, n):
    value = jnp.int32(table[0])
    for i, item in enumerate(table):
        value = jnp.where(n == i, item, value)
    return value


def kernel(
    lengths_hbm, shard_map_hbm, attn, teacher, codes_hbm, scales_hbm, offsets_hbm, out,
    lengths, shard_map, scales, offsets, a, codes, parts, acc, rowsum, tz, tf, t_land, target, grads, rs_land,
    loc, ays, acs, ayr, azr, acr, ws, w0r, wxr, whr, scs, scr,
    tps, tpr, tfr, tmr, tys, tyr, tcs, tcr, hello, rss, rsr, ags, agr,
):
    dp = lax.axis_index("dp")
    me = lax.axis_index("tensor")
    zh, y = me // NY, me % NY
    zl, x, core = dp // 8, dp // 2 % 4, dp % 2
    prim_core = zh // 2
    prim = core == prim_core
    sec = core != prim_core
    zp = 3 - zh
    zq = zh + 1 - 2 * (zh % 2)
    zr = 3 - zq

    def dev(zl_, x_, core_, zh_, y_):
        return (zl_ * 8 + x_ * 2 + core_, zh_ * NY + y_)

    y_nb = (dev(zl, x, core, zh, (y + 1) % NY), dev(zl, x, core, zh, (y + NY - 1) % NY))
    x_nb = (dev(zl, (x + 1) % 4, core, zh, y), dev(zl, (x + 3) % 4, core, zh, y))
    on_chip = dev(zl, x, 1 - core, zh, y)
    zl_nb = dev(1 - zl, x, core, zh, y)
    mate = dev(zl, x, core, zq, y)
    partner = dev(zl, x, core, zp, y)
    cross = dev(zl, x, 1 - core, zp, y)

    def remote(src, dst, ssem, rsem, to):
        return pltpu.make_async_remote_copy(
            src_ref=src, dst_ref=dst, send_sem=ssem, recv_sem=rsem,
            device_id=to, device_id_type=MESH,
        )

    def wait_all(ref, sem):
        pltpu.make_async_copy(ref, ref, sem).wait()

    barrier = pltpu.get_barrier_semaphore()
    for to in y_nb + x_nb + (on_chip, zl_nb, mate, partner, cross):
        pl.semaphore_signal(barrier, 1, device_id=to, device_id_type=MESH)

    def say_hello(r):
        for to in x_nb + (on_chip, zl_nb, cross):
            pl.semaphore_signal(hello.at[r], 1, device_id=to, device_id_type=MESH)

    def hear_hello(r):
        pl.semaphore_wait(hello.at[r], 5)
        if r + 1 < HELLOS:
            say_hello(r + 1)

    def plane_cols(z):
        return teacher.at[:, pl.ds(pl.multiple_of(z * NY * C, C), NY * C)]

    get_attn = pltpu.make_async_copy(attn, a.at[me], loc.at[0])
    get_codes = pltpu.make_async_copy(codes_hbm, codes, loc.at[1])
    get_scales = pltpu.make_async_copy(scales_hbm, scales, loc.at[2])
    get_offsets = pltpu.make_async_copy(offsets_hbm, offsets, loc.at[3])
    get_lengths = pltpu.make_async_copy(lengths_hbm, lengths, loc.at[4])
    get_map = pltpu.make_async_copy(shard_map_hbm, shard_map, loc.at[5])
    get_t = (
        pltpu.make_async_copy(plane_cols(zh), tz.at[0, zh], loc.at[6]),
        pltpu.make_async_copy(plane_cols(zp), tz.at[1, zh], loc.at[7]),
    )
    own_t = pltpu.make_async_copy(
        tz.at[:, :, :, pl.ds(pl.multiple_of(y * C, C), C)], t_land.at[:, y], loc.at[8]
    )

    @pl.when(prim)
    def _():
        for c in (get_attn, get_codes, get_scales, get_offsets) + get_t:
            c.start()

    get_lengths.start()
    get_map.start()
    acc[...] = jnp.zeros_like(acc)
    rowsum[...] = jnp.zeros_like(rowsum)
    pl.semaphore_wait(barrier, 9)

    group_iota = lax.broadcasted_iota(jnp.int32, (GROUPS, C), 0)
    feat_half = lax.broadcasted_iota(jnp.int32, (GROUPS, C), 1) // 128

    def use(slot):
        block = a[slot]
        halves = []
        for h in range(2):
            rows = pl.ds(pl.multiple_of(slot * C + h * 128, 128), 128)
            g = pl.ds(2 * slot + h, 1)
            piece = codes[rows, :]
            halves.append((piece.astype(F32) * scales[g, :] - offsets[g, :]).astype(BF16))
            parts[2 * slot + h] = jnp.dot(
                block[:, h * 128 : (h + 1) * 128], piece, preferred_element_type=F32
            )
        weight = jnp.concatenate(halves, axis=0)
        acc[...] += jnp.dot(block, weight, preferred_element_type=F32)
        pick = (group_iota == 2 * slot + feat_half).astype(BF16)
        rowsum[...] += lax.dot_general(
            pick, block, (((1,), (1,)), ((), ())), preferred_element_type=F32
        )

    def make_target():
        get_map.wait()
        lane = lax.broadcasted_iota(jnp.int32, (8, T), 1)
        where_to = jnp.zeros((8, T), jnp.int32)
        for j in range(NT):
            where_to = jnp.where(
                lane // 8 == j % NY * NZ + j // NY, shard_map[j] * 8 + lane % 8, where_to
            )
        row = lax.broadcasted_iota(jnp.int32, (T, T), 0)
        perm = (row == where_to[:1, :]).astype(F32).astype(BF16)
        arrived = t_land[0].astype(F32).reshape(T, C).astype(BF16)
        target[...] = jnp.dot(perm, arrived, preferred_element_type=F32)

    def slot_of(s, k, d):
        z = jnp.where(k == 0, zh, jnp.where(k == 1, zp, jnp.where(k == 2, zq, zr)))
        return z * NY + ((y + NY - s) % NY if d == 0 else (y + s) % NY)

    def y_full(s, k, d):
        ref = a.at[slot_of(s, k, d)]
        return remote(ref, ref, ays, ayr.at[s, k], y_nb[d])

    def y_half(k, d):
        ref = a.at[slot_of(3, k, d), pl.ds(d * 128, 128)]
        return remote(ref, ref, ays, ayr.at[3, k], y_nb[d])

    def share(s, k, d):
        ref = a.at[slot_of(s, k, d)]
        return remote(ref, ref, acs, acr.at[s, k], on_chip)

    def ty_copy(i):
        yt = (y + i) % NY
        return remote(
            tz.at[:, :, :, pl.ds(pl.multiple_of(yt * C, C), C)], t_land.at[:, y],
            tys, tyr, dev(zl, x, core, zh, yt),
        )

    def primary():
        get_attn.wait()
        remote(a.at[me], a.at[me], ays, azr.at[1], mate).start()
        for d in range(2):
            y_full(0, 0, d).start()
        share(0, 0, 0).start()
        remote(plane_cols(zq), tz.at[0, zh], tps, tmr, mate).start()
        remote(plane_cols(zr), tz.at[1, zh], tps, tmr, mate).start()
        get_codes.wait()
        get_scales.wait()
        get_offsets.wait()

        @pl.loop(0, len(EVENTS))
        def _(n):
            s = entry([e[0] for e in EVENTS], n)
            k = entry([e[1] for e in EVENTS], n)

            @pl.when(s == 0)
            def _():
                @pl.when(k == 1)
                def _():
                    wait_all(a.at[0], azr.at[0])
                    ref = a.at[slot_of(0, 1, 0)]
                    remote(ref, ref, ays, azr.at[2], mate).start()

                @pl.when(k > 1)
                def _():
                    wait_all(a.at[0], azr.at[k - 1])

                @pl.when(k > 0)
                def _():
                    y_full(0, k, 0).start()
                    y_full(0, k, 1).start()
                    share(0, k, 0).start()

            @pl.when((s > 0) & (s < 4))
            def _():
                wait_all(a.at[pl.ds(0, 2)], ayr.at[s - 1, k])
                for d in range(2):
                    @pl.when(s < 3)
                    def _():
                        y_full(s, k, d).start()

                    @pl.when(s == 3)
                    def _():
                        y_half(k, d).start()

                for d in range(2):
                    share(s, k, d).start()

            @pl.when(s == 4)
            def _():
                wait_all(a.at[0], ayr.at[3, k])
                share(4, k, 0).start()

            for r in range(HELLOS):
                @pl.when(n == 2 + 3 * r)
                def _():
                    hear_hello(r)

            @pl.when(n == 9)
            def _():
                wait_all(tf, tfr)
                remote(tf.at[0], tz.at[0, zp], tps, tmr, mate).start()
                remote(tf.at[1], tz.at[1, zp], tps, tmr, mate).start()

            @pl.when(n == 15)
            def _():
                for c in get_t:
                    c.wait()
                wait_all(tf, tpr)
                wait_all(tz.at[0], tmr)
                own_t.start()

                @pl.loop(1, NY)
                def _(i):
                    ty_copy(i).start()

            @pl.when(n == 18)
            def _():
                own_t.wait()
                wait_all(t_land.at[:, pl.ds(0, NY - 1)], tyr)
                remote(t_land.at[1], t_land.at[0], tcs, tcr, on_chip).start()

            use(slot_of(s, k, 0))

            @pl.when((s > 0) & (s < 4))
            def _():
                use(slot_of(s, k, 1))

        make_target()

    def y_of(m):
        return (y + NY + (m + 1) // 2 * (1 - 2 * (m % 2))) % NY

    def code_rows(q, m, h, first, count):
        return pl.ds(pl.multiple_of((q * NY + y_of(m)) * C + h * 128 + first, 64), count)

    def piece_of(e):
        m = entry(PIECE, e)
        direct = entry(DIRECT, e)
        return m, direct, jnp.where(direct == 1, zl, 1 - zl)

    def send_direct(m):
        rows = code_rows(x, m, zl, 0, 128)
        first = 2 * m - 1 + (m == 0) if isinstance(m, int) else 2 * m - 1
        remote(codes_hbm.at[rows], codes.at[rows], ws, w0r.at[first], cross).start()

    def secondary():
        remote(attn, a.at[me], ays, azr.at[0], partner).start()
        for m in range(AHEAD):
            send_direct(m)

        @pl.loop(0, 16 + LAG2)
        def _(n):
            @pl.when(n < 16)
            def _():
                m, direct, h = piece_of(n)
                rows = code_rows(x, m, h, 0, 128)
                wait_all(codes.at[pl.ds(0, 128)], w0r.at[n])
                for to in x_nb:
                    remote(codes.at[rows], codes.at[rows], ws, wxr.at[n], to).start()

                @pl.when(direct == 1)
                def _():
                    later = jnp.where(m < 7, 2 * m + 2, 15)
                    remote(codes.at[rows], codes.at[rows], ws, w0r.at[later], zl_nb).start()

                    @pl.when(m + AHEAD < NY)
                    def _():
                        send_direct(m + AHEAD)

            @pl.when(n == 3)
            def _():
                remote(scales_hbm, scales, scs.at[0], scr.at[0], cross).start()
                remote(offsets_hbm, offsets, scs.at[1], scr.at[1], cross).start()

            @pl.when(n == 6)
            def _():
                remote(plane_cols(zr), tf.at[0], tps, tfr, partner).start()
                remote(plane_cols(zq), tf.at[1], tps, tfr, partner).start()

            @pl.when(n == 9)
            def _():
                remote(plane_cols(zp), tz.at[0, zh], tps, tpr, partner).start()
                remote(plane_cols(zh), tz.at[1, zh], tps, tpr, partner).start()

            e1 = n - LAG1

            @pl.when((e1 >= 0) & (e1 < 16))
            def _():
                m, direct, h = piece_of(e1)
                wait_all(codes.at[pl.ds(0, 256)], wxr.at[e1])
                for d in range(2):
                    q = (x + 3) % 4 if d == 0 else (x + 1) % 4
                    rows = code_rows(q, m, h, d * 64, 64)
                    remote(codes.at[rows], codes.at[rows], ws, whr.at[e1], x_nb[d]).start()

            for r in range(HELLOS):
                @pl.when(n == 2 + 4 * r)
                def _():
                    hear_hello(r)

            e2 = n - LAG2

            @pl.when(e2 >= 0)
            def _():
                m, direct, h = piece_of(e2)
                wait_all(codes.at[pl.ds(0, 128)], whr.at[e2])

                @pl.when(direct == 0)
                def _():
                    s = (m + 1) // 2

                    @pl.when(m == 0)
                    def _():
                        wait_all(scales, scr.at[0])
                        wait_all(offsets, scr.at[1])

                    @pl.when((m == 0) | (m == 7))
                    def _():
                        @pl.loop(0, 4)
                        def _(k):
                            wait_all(a.at[0], acr.at[s, k])

                    @pl.when((m % 2 == 1) & (m < 7))
                    def _():
                        @pl.loop(0, 4)
                        def _(k):
                            wait_all(a.at[pl.ds(0, 2)], acr.at[s, k])

                    @pl.loop(0, 4)
                    def _(q):
                        use(q * NY + y_of(m))

        wait_all(t_land.at[0], tcr)
        make_target()

    say_hello(0)

    @pl.when(prim)
    def _():
        primary()

    @pl.when(sec)
    def _():
        secondary()

    get_lengths.wait()
    total = lengths[0]
    for i in range(1, 32):
        total = total + lengths[i]
    first_seq = 2 * (zl * 8 + x * 2 + prim_core)
    token = lax.broadcasted_iota(jnp.int32, (T, C), 0)
    limit = jnp.where(token < SEQ, lengths[first_seq], lengths[first_seq + 1] + SEQ)
    live = (token < limit).astype(F32)
    cot16 = (2.0 * (acc[...] - target[...]) * live / total.astype(F32)).astype(BF16)
    acc[...] = cot16.astype(F32)

    rs = rowsum[...]
    hi = rs.astype(BF16)
    rest = rs - hi.astype(F32)
    mid = rest.astype(BF16)
    low = (rest - mid.astype(F32)).astype(BF16)
    offs = jnp.dot(hi, cot16, preferred_element_type=F32)
    offs += jnp.dot(mid, cot16, preferred_element_type=F32)
    offs += jnp.dot(low, cot16, preferred_element_type=F32)
    grads[pl.ds(8, 8)] = -offs.reshape(8, 8, C)

    columns_at = jnp.where(prim, zh, zp) * NY + y
    giver = jnp.where(prim, 0, 8) + zl * 4 + x

    def rs_send(c):
        @pl.when(sec | (c != dp))
        def _():
            remote(grads.at[c], rs_land.at[giver], rss, rsr, (c, columns_at)).start()

    @pl.loop(8, 16)
    def _(c):
        rs_send(c)

    @pl.loop(0, 8)
    def _(c):
        for q in range(8):
            prod = parts[c * 8 + q] * acc[...]
            grads[c, pl.ds(q, 1), :] = jnp.sum(prod, axis=0, keepdims=True)
        rs_send(c)

    @pl.when(prim)
    def _():
        rs_land[giver] = grads[dp]
        wait_all(rs_land.at[pl.ds(0, NDP - 1)], rsr)

    @pl.when(sec)
    def _():
        wait_all(rs_land, rsr)

    out[dp] = jnp.sum(rs_land[...], axis=0)

    @pl.loop(0, NDP)
    def _(c):
        @pl.when(c != dp)
        def _():
            remote(out.at[dp], out.at[dp], ags, agr, (c, me)).start()

    wait_all(tz.at[0], tps)

    @pl.when(prim)
    def _():
        wait_all(a.at[pl.ds(0, 30)], ays)
        wait_all(a, acs)
        wait_all(t_land.at[:, pl.ds(0, NY - 1)], tys)
        wait_all(t_land.at[0], tcs)
        wait_all(rs_land.at[pl.ds(0, NDP - 1)], rss)

    @pl.when(sec)
    def _():
        wait_all(a.at[0], ays)
        wait_all(codes, ws)
        wait_all(scales, scs.at[0])
        wait_all(offsets, scs.at[1])
        wait_all(rs_land, rss)

    wait_all(out.at[pl.ds(0, NDP - 1)], ags)
    wait_all(out.at[pl.ds(0, NDP - 1)], agr)


def per_device(attn_out, teacher, int_codes, scales, offsets, lengths, shard_map):
    dma = pltpu.SemaphoreType.DMA
    hbm = pl.BlockSpec(memory_space=pltpu.HBM)
    out = pl.pallas_call(
        kernel,
        out_shape=pltpu.VMEM((NDP, 8, C), F32),
        in_specs=[hbm] * 7,
        out_specs=pl.BlockSpec(memory_space=pltpu.VMEM),
        scratch_shapes=[
            pltpu.SMEM((32,), jnp.int32),
            pltpu.SMEM((32,), jnp.int32),
            pltpu.VMEM((GROUPS, C), F32),
            pltpu.VMEM((GROUPS, C), F32),
            pltpu.VMEM((NT, T, C), BF16),
            pltpu.VMEM((NT * C, C), BF16),
            pltpu.VMEM((GROUPS, T, C), F32),
            pltpu.VMEM((T, C), F32),
            pltpu.VMEM((GROUPS, T), F32),
            pltpu.VMEM((2, NZ, 8, NY * C), BF16),
            pltpu.VMEM((2, 8, NY * C), BF16),
            pltpu.VMEM((2, NY, NZ, 8, C), BF16),
            pltpu.VMEM((T, C), F32),
            pltpu.VMEM((NDP, 8, C), F32),
            pltpu.VMEM((NDP, 8, C), F32),
            dma((9,)),
            dma(()), dma(()), dma((4, 4)), dma((3,)), dma((5, 4)),
            dma(()), dma((16,)), dma((16,)), dma((16,)), dma((2,)), dma((2,)),
            dma(()), dma(()), dma(()), dma(()), dma(()), dma(()), dma(()), dma(()),
            pltpu.SemaphoreType.REGULAR((HELLOS,)),
            dma(()), dma(()), dma(()), dma(()),
        ],
        compiler_params=pltpu.CompilerParams(
            collective_id=0, has_side_effects=True, vmem_limit_bytes=63 << 20
        ),
        cost_estimate=pl.CostEstimate(
            flops=3 * 2 * T * 8192 * C, bytes_accessed=6 << 20, transcendentals=0
        ),
    )(lengths, shard_map, attn_out, teacher, int_codes, scales, offsets)
    flat = out.reshape(128, C)
    return flat[:64], flat[64:]


def solution(mesh):
    in_specs = (
        P("dp", "tensor"),
        P(("dp", "tensor"), None),
        P(None, "tensor"),
        P(None, "tensor"),
        P(None, "tensor"),
        P(),
        P(),
    )
    out_specs = (P(None, "tensor"), P(None, "tensor"))
    return jax.shard_map(
        per_device, mesh=mesh, in_specs=in_specs, out_specs=out_specs, check_vma=False
    )
```

```python
import jax
import jax.numpy as jnp
from jax import lax
from jax.experimental import pallas as pl
from jax.experimental.pallas import tpu as pltpu
from jax.sharding import PartitionSpec as P

SEQ = 128
T = 256
C = 256
NY, NZ = 8, 4
NT = NY * NZ
NDP = 16
GROUPS = 64
F32, BF16 = jnp.float32, jnp.bfloat16
MESH = pl.DeviceIdType.MESH
EVENTS = [
    0, 1, 8, 9, 4, 2, 5, 3, 12, 16, 10, 13, 6, 11, 7, 17, 20, 14, 18, 15,
    21, 19, 22, 24, 25, 23, 28, 26, 29, 27, 30, 32, 33, 31, 36, 34, 37, 35, 38, 39,
]
PIECE = [0, 1, 0, 2, 1, 3, 2, 4, 3, 5, 4, 6, 5, 7, 6, 7]
DIRECT = [1, 1, 0, 1, 0, 1, 0, 1, 0, 1, 0, 1, 0, 1, 0, 0]
LAG1, LAG2 = 4, 8
BLOCK_AT = [-1] * 12 + [0, -1, 1, -1, 2, -1, 3, -1, 4, 5, 6, 7]
AHEAD = 3
TR_AT, TP_AT = 7, 9
TY_AT, TC_AT = 28, 38
HELLOS = 4


def entry(table, n):
    value = jnp.int32(table[0])
    for i, item in enumerate(table):
        value = jnp.where(n == i, item, value)
    return value


def kernel(
    lengths_hbm, shard_map_hbm, attn, teacher, codes_hbm, scales_hbm, offsets_hbm, out,
    lengths, shard_map, scales, offsets, a, codes, parts, acc, rowsum, tz, t_land, target, grads, rs_land,
    loc, ays, acs, ayr, azr, acr, ws, w0r, wxr, whr, scs, scr,
    tps, tpr, tmr, tys, tyr, tcs, tcr, hello, rss, rsr, ags, agr,
):
    dp = lax.axis_index("dp")
    me = lax.axis_index("tensor")
    zh, y = me // NY, me % NY
    zl, x, core = dp // 8, dp // 2 % 4, dp % 2
    prim_core = zh // 2
    prim = core == prim_core
    sec = core != prim_core
    zp = 3 - zh
    zq = zh + 1 - 2 * (zh % 2)
    zr = 3 - zq

    def dev(zl_, x_, core_, zh_, y_):
        return (zl_ * 8 + x_ * 2 + core_, zh_ * NY + y_)

    y_nb = (dev(zl, x, core, zh, (y + 1) % NY), dev(zl, x, core, zh, (y + NY - 1) % NY))
    x_nb = (dev(zl, (x + 1) % 4, core, zh, y), dev(zl, (x + 3) % 4, core, zh, y))
    on_chip = dev(zl, x, 1 - core, zh, y)
    zl_nb = dev(1 - zl, x, core, zh, y)
    mate = dev(zl, x, core, zq, y)
    partner = dev(zl, x, core, zp, y)
    cross = dev(zl, x, 1 - core, zp, y)

    def remote(src, dst, ssem, rsem, to):
        return pltpu.make_async_remote_copy(
            src_ref=src, dst_ref=dst, send_sem=ssem, recv_sem=rsem,
            device_id=to, device_id_type=MESH,
        )

    def wait_all(ref, sem):
        pltpu.make_async_copy(ref, ref, sem).wait()

    near = y_nb + x_nb + (on_chip, zl_nb, mate, partner, cross)
    barrier = pltpu.get_barrier_semaphore()
    for to in near:
        pl.semaphore_signal(barrier, 1, device_id=to, device_id_type=MESH)

    def say_hello(r):
        for to in near:
            pl.semaphore_signal(hello.at[r], 1, device_id=to, device_id_type=MESH)

    def hear_hello(r):
        pl.semaphore_wait(hello.at[r], 9)
        if r + 1 < HELLOS:
            say_hello(r + 1)

    def plane_cols(z):
        return teacher.at[:, pl.ds(pl.multiple_of(z * NY * C, C), NY * C)]

    get_attn = pltpu.make_async_copy(attn, a.at[me], loc.at[0])
    get_codes = pltpu.make_async_copy(codes_hbm, codes, loc.at[1])
    get_scales = pltpu.make_async_copy(scales_hbm, scales, loc.at[2])
    get_offsets = pltpu.make_async_copy(offsets_hbm, offsets, loc.at[3])
    get_lengths = pltpu.make_async_copy(lengths_hbm, lengths, loc.at[4])
    get_map = pltpu.make_async_copy(shard_map_hbm, shard_map, loc.at[5])
    get_t = (
        pltpu.make_async_copy(plane_cols(zh), tz.at[0, zh], loc.at[6]),
        pltpu.make_async_copy(plane_cols(zp), tz.at[1, zh], loc.at[7]),
    )
    own_t = pltpu.make_async_copy(
        tz.at[:, :, :, pl.ds(pl.multiple_of(y * C, C), C)], t_land.at[:, y], loc.at[8]
    )

    @pl.when(prim)
    def _():
        for c in (get_attn, get_codes, get_scales, get_offsets) + get_t:
            c.start()

    get_lengths.start()
    get_map.start()
    acc[...] = jnp.zeros_like(acc)
    rowsum[...] = jnp.zeros_like(rowsum)
    pl.semaphore_wait(barrier, 9)

    group_iota = lax.broadcasted_iota(jnp.int32, (GROUPS, C), 0)
    feat_half = lax.broadcasted_iota(jnp.int32, (GROUPS, C), 1) // 128

    def use(slot):
        block = a[slot]
        halves = []
        for h in range(2):
            rows = pl.ds(pl.multiple_of(slot * C + h * 128, 128), 128)
            g = pl.ds(2 * slot + h, 1)
            piece = codes[rows, :]
            halves.append((piece.astype(F32) * scales[g, :] - offsets[g, :]).astype(BF16))
            parts[2 * slot + h] = jnp.dot(
                block[:, h * 128 : (h + 1) * 128], piece, preferred_element_type=F32
            )
        weight = jnp.concatenate(halves, axis=0)
        acc[...] += jnp.dot(block, weight, preferred_element_type=F32)
        pick = (group_iota == 2 * slot + feat_half).astype(BF16)
        rowsum[...] += lax.dot_general(
            pick, block, (((1,), (1,)), ((), ())), preferred_element_type=F32
        )

    def make_target():
        get_map.wait()
        lane = lax.broadcasted_iota(jnp.int32, (8, T), 1)
        where_to = jnp.zeros((8, T), jnp.int32)
        for j in range(NT):
            where_to = jnp.where(
                lane // 8 == j % NY * NZ + j // NY, shard_map[j] * 8 + lane % 8, where_to
            )
        row = lax.broadcasted_iota(jnp.int32, (T, T), 0)
        perm = (row == where_to[:1, :]).astype(F32).astype(BF16)
        arrived = t_land[0].astype(F32).reshape(T, C).astype(BF16)
        target[...] = jnp.dot(perm, arrived, preferred_element_type=F32)

    def plane_of(k):
        return jnp.where(k == 0, zh, jnp.where(k == 1, zp, jnp.where(k == 2, zq, zr)))

    def index_of(z):
        return jnp.where(z == zh, 0, jnp.where(z == zp, 1, jnp.where(z == zq, 2, 3)))

    def slot_of(s, k, d):
        return plane_of(k) * NY + ((y + NY - s) % NY if d == 0 else (y + s) % NY)

    def half_of(s, kk, d):
        return a.at[slot_of(s, kk // 2, d), pl.ds(pl.multiple_of(kk % 2 * 128, 128), 128)]

    def y_full(s, kk, d):
        ref = half_of(s, kk, d)
        return remote(ref, ref, ays, ayr.at[s, kk], y_nb[d])

    def y_part(kk, d):
        rows = pl.ds(pl.multiple_of(kk % 2 * 128 + d * 64, 64), 64)
        ref = a.at[slot_of(3, kk // 2, d), rows]
        return remote(ref, ref, ays, ayr.at[3, kk], y_nb[d])

    def share(s, k, d):
        ref = a.at[slot_of(s, k, d)]
        return remote(ref, ref, acs, acr.at[s, k], on_chip)

    def ty_copy(i):
        yt = (y + i) % NY
        return remote(
            tz.at[:, :, :, pl.ds(pl.multiple_of(yt * C, C), C)], t_land.at[:, y],
            tys, tyr, dev(zl, x, core, zh, yt),
        )

    def primary():
        get_attn.wait()
        for h in range(2):
            ref = half_of(0, h, 0)
            remote(ref, ref, ays, azr.at[1, h], mate).start()
            for d in range(2):
                y_full(0, h, d).start()
        share(0, 0, 0).start()
        remote(plane_cols(zq), tz.at[0, zh], tps, tmr, mate).start()
        remote(plane_cols(zr), tz.at[1, zh], tps, tmr, mate).start()
        get_codes.wait()
        get_scales.wait()
        get_offsets.wait()

        @pl.loop(0, len(EVENTS))
        def _(n):
            code = entry(EVENTS, n)
            s, kk = code // 8, code % 8
            k, h = kk // 2, kk % 2

            @pl.when(s == 0)
            def _():
                @pl.when(k > 0)
                def _():
                    wait_all(a.at[0, pl.ds(0, 128)], azr.at[k - 1, h])

                    @pl.when(k == 1)
                    def _():
                        ref = half_of(0, kk, 0)
                        remote(ref, ref, ays, azr.at[2, h], mate).start()

                    y_full(0, kk, 0).start()
                    y_full(0, kk, 1).start()

                    @pl.when(h == 1)
                    def _():
                        share(0, k, 0).start()

            @pl.when((s > 0) & (s < 4))
            def _():
                wait_all(a.at[0], ayr.at[s - 1, kk])
                for d in range(2):
                    @pl.when(s < 3)
                    def _():
                        y_full(s, kk, d).start()

                    @pl.when(s == 3)
                    def _():
                        y_part(kk, d).start()

                @pl.when(h == 1)
                def _():
                    for d in range(2):
                        share(s, k, d).start()

            @pl.when(s == 4)
            def _():
                wait_all(a.at[0, pl.ds(0, 128)], ayr.at[3, kk])

                @pl.when(h == 1)
                def _():
                    share(4, k, 0).start()

            for r in range(HELLOS):
                @pl.when(n == 4 + 6 * r)
                def _():
                    hear_hello(r)

            @pl.when(n == TY_AT)
            def _():
                for c in get_t:
                    c.wait()
                wait_all(tz.at[0, pl.ds(0, 2)], tpr)
                wait_all(tz.at[0], tmr)
                own_t.start()

                @pl.loop(1, NY)
                def _(i):
                    ty_copy(i).start()

            @pl.when(n == TC_AT)
            def _():
                own_t.wait()
                wait_all(t_land.at[:, pl.ds(0, NY - 1)], tyr)
                remote(t_land.at[1], t_land.at[0], tcs, tcr, on_chip).start()
                make_target()

            @pl.when(h == 1)
            def _():
                use(slot_of(s, k, 0))

            @pl.when((h == 1) & (s > 0) & (s < 4))
            def _():
                use(slot_of(s, k, 1))

    def y_of(m):
        return (y + NY + (m + 1) // 2 * (1 - 2 * (m % 2))) % NY

    def code_rows(q, m, h, first, count):
        return pl.ds(pl.multiple_of((q * NY + y_of(m)) * C + h * 128 + first, 64), count)

    def piece_of(e):
        m = entry(PIECE, e)
        direct = entry(DIRECT, e)
        return m, direct, jnp.where(direct == 1, zl, 1 - zl)

    def send_direct(m):
        rows = code_rows(x, m, zl, 0, 128)
        first = 2 * m - 1 + (m == 0) if isinstance(m, int) else 2 * m - 1
        remote(codes_hbm.at[rows], codes.at[rows], ws, w0r.at[first], cross).start()

    def secondary():
        for h in range(2):
            rows = pl.ds(h * 128, 128)
            remote(attn.at[rows], a.at[me, rows], ays, azr.at[0, h], partner).start()
        for m in range(AHEAD):
            send_direct(m)

        @pl.loop(0, 16 + LAG2)
        def _(n):
            @pl.when(n < 16)
            def _():
                m, direct, h = piece_of(n)
                rows = code_rows(x, m, h, 0, 128)
                wait_all(codes.at[pl.ds(0, 128)], w0r.at[n])
                for to in x_nb:
                    remote(codes.at[rows], codes.at[rows], ws, wxr.at[n], to).start()

                @pl.when((direct == 1) & (m < 7))
                def _():
                    remote(codes.at[rows], codes.at[rows], ws, w0r.at[2 * m + 2], zl_nb).start()

                    @pl.when(m + AHEAD < NY)
                    def _():
                        send_direct(m + AHEAD)

                    @pl.when(m + AHEAD == 7)
                    def _():
                        last = code_rows(x, 7, zl, 0, 128)
                        both = dev(1 - zl, x, 1 - core, zp, y)
                        remote(codes_hbm.at[last], codes.at[last], ws, w0r.at[15], both).start()

            @pl.when(n == 1)
            def _():
                @pl.when(zl == 0)
                def _():
                    remote(scales_hbm, scales, scs, scr.at[0], cross).start()

                @pl.when(zl == 1)
                def _():
                    remote(offsets_hbm, offsets, scs, scr.at[1], cross).start()

            @pl.when(n == 6)
            def _():
                @pl.when(zl == 0)
                def _():
                    wait_all(scales, scr.at[0])
                    remote(scales, scales, scs, scr.at[0], zl_nb).start()

                @pl.when(zl == 1)
                def _():
                    wait_all(offsets, scr.at[1])
                    remote(offsets, offsets, scs, scr.at[1], zl_nb).start()

            @pl.when(n == TR_AT)
            def _():
                other = dev(zl, x, core, zr, y)
                remote(plane_cols(zr), tz.at[0, zh], tps, tmr, other).start()
                remote(plane_cols(zq), tz.at[1, zh], tps, tmr, other).start()

            @pl.when(n == TP_AT)
            def _():
                remote(plane_cols(zp), tz.at[0, zh], tps, tpr, partner).start()
                remote(plane_cols(zh), tz.at[1, zh], tps, tpr, partner).start()

            e1 = n - LAG1

            @pl.when((e1 >= 0) & (e1 < 16))
            def _():
                m, direct, h = piece_of(e1)
                wait_all(codes.at[pl.ds(0, 256)], wxr.at[e1])
                for d in range(2):
                    q = (x + 3) % 4 if d == 0 else (x + 1) % 4
                    rows = code_rows(q, m, h, d * 64, 64)
                    remote(codes.at[rows], codes.at[rows], ws, whr.at[e1], x_nb[d]).start()

            for r in range(HELLOS):
                @pl.when(n == 2 + 4 * r)
                def _():
                    hear_hello(r)

            m = entry(BLOCK_AT, n)
            s = (m + 1) // 2

            @pl.when(m == 7)
            def _():
                wait_all(t_land.at[0], tcr)
                make_target()

                for i in (0, 1, 3):
                    q = (x + i) % 4
                    wait_all(a.at[0], acr.at[4, index_of(q)])
                    use(q * NY + y_of(7))

            e2 = n - LAG2

            @pl.when(e2 >= 0)
            def _():
                wait_all(codes.at[pl.ds(0, 128)], whr.at[e2])

            @pl.when(m == 7)
            def _():
                q = (x + 2) % 4
                wait_all(a.at[0], acr.at[4, index_of(q)])
                use(q * NY + y_of(7))

            @pl.when((m >= 0) & (m < 7))
            def _():
                @pl.when(m == 0)
                def _():
                    @pl.when(zl == 1)
                    def _():
                        wait_all(scales, scr.at[0])

                    @pl.when(zl == 0)
                    def _():
                        wait_all(offsets, scr.at[1])

                @pl.loop(0, 4)
                def _(k):
                    @pl.when(m == 0)
                    def _():
                        wait_all(a.at[0], acr.at[0, k])

                    @pl.when(m % 2 == 1)
                    def _():
                        wait_all(a.at[pl.ds(0, 2)], acr.at[s, k])

                    use(plane_of(k) * NY + y_of(m))

    say_hello(0)

    @pl.when(prim)
    def _():
        primary()

    @pl.when(sec)
    def _():
        secondary()

    get_lengths.wait()
    total = lengths[0]
    for i in range(1, 32):
        total = total + lengths[i]
    first_seq = 2 * (zl * 8 + x * 2 + prim_core)
    token = lax.broadcasted_iota(jnp.int32, (T, C), 0)
    limit = jnp.where(token < SEQ, lengths[first_seq], lengths[first_seq + 1] + SEQ)
    live = (token < limit).astype(F32)
    cot16 = (2.0 * (acc[...] - target[...]) * live / total.astype(F32)).astype(BF16)
    acc[...] = cot16.astype(F32)

    rs = rowsum[...]
    hi = rs.astype(BF16)
    rest = rs - hi.astype(F32)
    mid = rest.astype(BF16)
    low = (rest - mid.astype(F32)).astype(BF16)
    offs = jnp.dot(hi, cot16, preferred_element_type=F32)
    offs += jnp.dot(mid, cot16, preferred_element_type=F32)
    offs += jnp.dot(low, cot16, preferred_element_type=F32)
    grads[pl.ds(8, 8)] = -offs.reshape(8, 8, C)

    columns_at = jnp.where(prim, zh, zp) * NY + y
    giver = jnp.where(prim, 0, 8) + zl * 4 + x

    def rs_send(c):
        @pl.when(sec | (c != dp))
        def _():
            remote(grads.at[c], rs_land.at[giver], rss, rsr, (c, columns_at)).start()

    @pl.loop(8, 16)
    def _(c):
        rs_send(c)

    @pl.loop(0, 8)
    def _(c):
        for q in range(8):
            prod = parts[c * 8 + q] * acc[...]
            grads[c, pl.ds(q, 1), :] = jnp.sum(prod, axis=0, keepdims=True)
        rs_send(c)

    @pl.when(prim)
    def _():
        rs_land[giver] = grads[dp]
        wait_all(rs_land.at[pl.ds(0, NDP - 1)], rsr)

    @pl.when(sec)
    def _():
        wait_all(rs_land, rsr)

    out[dp] = jnp.sum(rs_land[...], axis=0)

    @pl.loop(0, NDP)
    def _(c):
        @pl.when(c != dp)
        def _():
            remote(out.at[dp], out.at[dp], ags, agr, (c, me)).start()

    @pl.when(prim)
    def _():
        wait_all(tz.at[0, pl.ds(0, 2)], tps)
        wait_all(a.at[pl.ds(0, 30)], ays)
        wait_all(a, acs)
        wait_all(t_land.at[:, pl.ds(0, NY - 1)], tys)
        wait_all(t_land.at[0], tcs)
        wait_all(rs_land.at[pl.ds(0, NDP - 1)], rss)

    @pl.when(sec)
    def _():
        wait_all(tz.at[0], tps)
        wait_all(a.at[0], ays)
        wait_all(codes, ws)
        wait_all(target.at[pl.ds(0, 128)], scs)
        wait_all(rs_land, rss)

    wait_all(out.at[pl.ds(0, NDP - 1)], ags)
    wait_all(out.at[pl.ds(0, NDP - 1)], agr)


def per_device(attn_out, teacher, int_codes, scales, offsets, lengths, shard_map):
    dma = pltpu.SemaphoreType.DMA
    hbm = pl.BlockSpec(memory_space=pltpu.HBM)
    out = pl.pallas_call(
        kernel,
        out_shape=pltpu.VMEM((NDP, 8, C), F32),
        in_specs=[hbm] * 7,
        out_specs=pl.BlockSpec(memory_space=pltpu.VMEM),
        scratch_shapes=[
            pltpu.SMEM((32,), jnp.int32),
            pltpu.SMEM((32,), jnp.int32),
            pltpu.VMEM((GROUPS, C), F32),
            pltpu.VMEM((GROUPS, C), F32),
            pltpu.VMEM((NT, T, C), BF16),
            pltpu.VMEM((NT * C, C), BF16),
            pltpu.VMEM((GROUPS, T, C), F32),
            pltpu.VMEM((T, C), F32),
            pltpu.VMEM((GROUPS, T), F32),
            pltpu.VMEM((2, NZ, 8, NY * C), BF16),
            pltpu.VMEM((2, NY, NZ, 8, C), BF16),
            pltpu.VMEM((T, C), F32),
            pltpu.VMEM((NDP, 8, C), F32),
            pltpu.VMEM((NDP, 8, C), F32),
            dma((9,)),
            dma(()), dma(()), dma((4, 8)), dma((3, 2)), dma((5, 4)),
            dma(()), dma((16,)), dma((16,)), dma((16,)), dma(()), dma((2,)),
            dma(()), dma(()), dma(()), dma(()), dma(()), dma(()), dma(()),
            pltpu.SemaphoreType.REGULAR((HELLOS,)),
            dma(()), dma(()), dma(()), dma(()),
        ],
        compiler_params=pltpu.CompilerParams(
            collective_id=0, has_side_effects=True, vmem_limit_bytes=63 << 20
        ),
        cost_estimate=pl.CostEstimate(
            flops=3 * 2 * T * 8192 * C, bytes_accessed=6 << 20, transcendentals=0
        ),
    )(lengths, shard_map, attn_out, teacher, int_codes, scales, offsets)
    flat = out.reshape(128, C)
    return flat[:64], flat[64:]


def solution(mesh):
    in_specs = (
        P("dp", "tensor"),
        P(("dp", "tensor"), None),
        P(None, "tensor"),
        P(None, "tensor"),
        P(None, "tensor"),
        P(),
        P(),
    )
    out_specs = (P(None, "tensor"), P(None, "tensor"))
    return jax.shard_map(
        per_device, mesh=mesh, in_specs=in_specs, out_specs=out_specs, check_vma=False
    )
```

```python
import jax
import jax.numpy as jnp
from jax import lax
from jax.experimental import pallas as pl
from jax.experimental.pallas import tpu as pltpu
from jax.sharding import PartitionSpec as P

SEQ = 128
T = 256
C = 256
NY, NZ = 8, 4
NT = NY * NZ
NDP = 16
GROUPS = 64
F32, BF16 = jnp.float32, jnp.bfloat16
MESH = pl.DeviceIdType.MESH
EVENTS = [
    0, 1, 8, 9, 4, 2, 5, 3, 12, 16, 10, 13, 6, 11, 7, 17, 20, 14, 18, 15,
    21, 19, 22, 24, 25, 23, 28, 26, 29, 27, 30, 32, 33, 31, 36, 34, 37, 35, 38, 39,
]
PIECE = [0, 1, 0, 2, 1, 3, 2, 4, 3, 5, 4, 6, 5, 7, 6, 7]
DIRECT = [1, 1, 0, 1, 0, 1, 0, 1, 0, 1, 0, 1, 0, 1, 0, 0]
LAG1, LAG2 = 4, 8
BLOCK_AT = [-1] * 12 + [0, -1, 1, -1, 2, -1, 3, -1, 4, 5, 6, 7]
AHEAD = 3
TR_AT, TP_AT = 7, 9
TY_AT, TC_AT = 26, 36
HELLOS = 4


def entry(table, n):
    value = jnp.int32(table[0])
    for i, item in enumerate(table):
        value = jnp.where(n == i, item, value)
    return value


def kernel(
    lengths_hbm, shard_map_hbm, attn, teacher, codes_hbm, scales_hbm, offsets_hbm, out,
    lengths, shard_map, scales, offsets, a, codes, parts, acc, rowsum, tz, t_land, target, grads, rs_land,
    loc, ays, acs, qr, acr, ws, scs, scr,
    tps, tpr, tmr, tys, tyr, tcs, tcr, hello, rss, rsr, ags, agr,
):
    dp = lax.axis_index("dp")
    me = lax.axis_index("tensor")
    zh, y = me // NY, me % NY
    zl, x, core = dp // 8, dp // 2 % 4, dp % 2
    prim_core = zh // 2
    prim = core == prim_core
    sec = core != prim_core
    zp = 3 - zh
    zq = zh + 1 - 2 * (zh % 2)
    zr = 3 - zq

    def dev(zl_, x_, core_, zh_, y_):
        return (zl_ * 8 + x_ * 2 + core_, zh_ * NY + y_)

    y_nb = (dev(zl, x, core, zh, (y + 1) % NY), dev(zl, x, core, zh, (y + NY - 1) % NY))
    x_nb = (dev(zl, (x + 1) % 4, core, zh, y), dev(zl, (x + 3) % 4, core, zh, y))
    on_chip = dev(zl, x, 1 - core, zh, y)
    zl_nb = dev(1 - zl, x, core, zh, y)
    mate = dev(zl, x, core, zq, y)
    partner = dev(zl, x, core, zp, y)
    cross = dev(zl, x, 1 - core, zp, y)

    def remote(src, dst, ssem, rsem, to):
        return pltpu.make_async_remote_copy(
            src_ref=src, dst_ref=dst, send_sem=ssem, recv_sem=rsem,
            device_id=to, device_id_type=MESH,
        )

    def wait_all(ref, sem):
        pltpu.make_async_copy(ref, ref, sem).wait()

    near = y_nb + x_nb + (on_chip, zl_nb, mate, partner, cross)
    barrier = pltpu.get_barrier_semaphore()
    for to in near:
        pl.semaphore_signal(barrier, 1, device_id=to, device_id_type=MESH)

    def say_hello(r):
        for to in near:
            pl.semaphore_signal(hello.at[r], 1, device_id=to, device_id_type=MESH)

    def hear_hello(r):
        pl.semaphore_wait(hello.at[r], 9)
        if r + 1 < HELLOS:
            say_hello(r + 1)

    def plane_cols(z):
        return teacher.at[:, pl.ds(pl.multiple_of(z * NY * C, C), NY * C)]

    get_attn = pltpu.make_async_copy(attn, a.at[me], loc.at[0])
    get_codes = pltpu.make_async_copy(codes_hbm, codes, loc.at[1])
    get_scales = pltpu.make_async_copy(scales_hbm, scales, loc.at[2])
    get_offsets = pltpu.make_async_copy(offsets_hbm, offsets, loc.at[3])
    get_lengths = pltpu.make_async_copy(lengths_hbm, lengths, loc.at[4])
    get_map = pltpu.make_async_copy(shard_map_hbm, shard_map, loc.at[5])
    get_t = (
        pltpu.make_async_copy(plane_cols(zh), tz.at[0, zh], loc.at[6]),
        pltpu.make_async_copy(plane_cols(zp), tz.at[1, zh], loc.at[7]),
    )
    own_t = pltpu.make_async_copy(
        tz.at[:, :, :, pl.ds(pl.multiple_of(y * C, C), C)], t_land.at[:, y], loc.at[8]
    )

    @pl.when(prim)
    def _():
        for c in (get_attn, get_codes, get_scales, get_offsets) + get_t:
            c.start()

    get_lengths.start()
    get_map.start()
    acc[...] = jnp.zeros_like(acc)
    rowsum[...] = jnp.zeros_like(rowsum)
    pl.semaphore_wait(barrier, 9)

    group_iota = lax.broadcasted_iota(jnp.int32, (GROUPS, C), 0)
    feat_half = lax.broadcasted_iota(jnp.int32, (GROUPS, C), 1) // 128

    def use(slot):
        block = a[slot]
        halves = []
        for h in range(2):
            rows = pl.ds(pl.multiple_of(slot * C + h * 128, 128), 128)
            g = pl.ds(2 * slot + h, 1)
            piece = codes[rows, :]
            halves.append((piece.astype(F32) * scales[g, :] - offsets[g, :]).astype(BF16))
            parts[2 * slot + h] = jnp.dot(
                block[:, h * 128 : (h + 1) * 128], piece, preferred_element_type=F32
            )
        weight = jnp.concatenate(halves, axis=0)
        acc[...] += jnp.dot(block, weight, preferred_element_type=F32)
        pick = (group_iota == 2 * slot + feat_half).astype(BF16)
        rowsum[...] += lax.dot_general(
            pick, block, (((1,), (1,)), ((), ())), preferred_element_type=F32
        )

    def make_target():
        get_map.wait()
        lane = lax.broadcasted_iota(jnp.int32, (8, T), 1)
        where_to = jnp.zeros((8, T), jnp.int32)
        for j in range(NT):
            where_to = jnp.where(
                lane // 8 == j % NY * NZ + j // NY, shard_map[j] * 8 + lane % 8, where_to
            )
        row = lax.broadcasted_iota(jnp.int32, (T, T), 0)
        perm = (row == where_to[:1, :]).astype(F32).astype(BF16)
        arrived = t_land[0].astype(F32).reshape(T, C).astype(BF16)
        target[...] = jnp.dot(perm, arrived, preferred_element_type=F32)

    def plane_of(k):
        return jnp.where(k == 0, zh, jnp.where(k == 1, zp, jnp.where(k == 2, zq, zr)))

    def index_of(z):
        return jnp.where(z == zh, 0, jnp.where(z == zp, 1, jnp.where(z == zq, 2, 3)))

    def slot_of(s, k, d):
        return plane_of(k) * NY + ((y + NY - s) % NY if d == 0 else (y + s) % NY)

    def half_of(s, kk, d):
        return a.at[slot_of(s, kk // 2, d), pl.ds(pl.multiple_of(kk % 2 * 128, 128), 128)]

    def y_full(s, kk, d):
        ref = half_of(s, kk, d)
        return remote(ref, ref, ays, qr.at[s * 8 + kk], y_nb[d])

    def y_part(kk, d):
        rows = pl.ds(pl.multiple_of(kk % 2 * 128 + d * 64, 64), 64)
        ref = a.at[slot_of(3, kk // 2, d), rows]
        return remote(ref, ref, ays, qr.at[24 + kk], y_nb[d])

    def share(s, k, d):
        ref = a.at[slot_of(s, k, d)]
        return remote(ref, ref, acs, acr.at[s, k], on_chip)

    def ty_copy(i):
        yt = (y + i) % NY
        return remote(
            tz.at[:, :, :, pl.ds(pl.multiple_of(yt * C, C), C)], t_land.at[:, y],
            tys, tyr, dev(zl, x, core, zh, yt),
        )

    def primary():
        get_attn.wait()
        for h in range(2):
            ref = half_of(0, h, 0)
            remote(ref, ref, ays, qr.at[34 + h], mate).start()
            for d in range(2):
                y_full(0, h, d).start()
        share(0, 0, 0).start()
        remote(plane_cols(zq), tz.at[0, zh], tps, tmr, mate).start()
        remote(plane_cols(zr), tz.at[1, zh], tps, tmr, mate).start()
        get_codes.wait()
        get_scales.wait()
        get_offsets.wait()

        @pl.loop(0, len(EVENTS))
        def _(n):
            code = entry(EVENTS, n)
            s, kk = code // 8, code % 8
            k, h = kk // 2, kk % 2

            @pl.when(s == 0)
            def _():
                @pl.when(k > 0)
                def _():
                    wait_all(a.at[0, pl.ds(0, 128)], qr.at[30 + 2 * k + h])

                    @pl.when(k == 1)
                    def _():
                        ref = half_of(0, kk, 0)
                        remote(ref, ref, ays, qr.at[36 + h], mate).start()

                    y_full(0, kk, 0).start()
                    y_full(0, kk, 1).start()

                    @pl.when(h == 1)
                    def _():
                        share(0, k, 0).start()

            @pl.when((s > 0) & (s < 4))
            def _():
                wait_all(a.at[0], qr.at[(s - 1) * 8 + kk])
                for d in range(2):
                    @pl.when(s < 3)
                    def _():
                        y_full(s, kk, d).start()

                    @pl.when(s == 3)
                    def _():
                        y_part(kk, d).start()

                @pl.when(h == 1)
                def _():
                    for d in range(2):
                        share(s, k, d).start()

            @pl.when(s == 4)
            def _():
                wait_all(a.at[0, pl.ds(0, 128)], qr.at[24 + kk])

                @pl.when(h == 1)
                def _():
                    share(4, k, 0).start()

            for r in range(HELLOS):
                @pl.when(n == 4 + 6 * r)
                def _():
                    hear_hello(r)

            @pl.when(n == TY_AT)
            def _():
                for c in get_t:
                    c.wait()
                wait_all(tz.at[0, pl.ds(0, 2)], tpr)
                wait_all(tz.at[0], tmr)
                own_t.start()

                @pl.loop(1, NY)
                def _(i):
                    ty_copy(i).start()

            @pl.when(n == TC_AT)
            def _():
                own_t.wait()
                wait_all(t_land.at[:, pl.ds(0, NY - 1)], tyr)
                remote(t_land.at[1], t_land.at[0], tcs, tcr, on_chip).start()
                make_target()

            @pl.when(h == 1)
            def _():
                use(slot_of(s, k, 0))

            @pl.when((h == 1) & (s > 0) & (s < 4))
            def _():
                use(slot_of(s, k, 1))

    def y_of(m):
        return (y + NY + (m + 1) // 2 * (1 - 2 * (m % 2))) % NY

    def code_rows(q, m, h, first, count):
        return pl.ds(pl.multiple_of((q * NY + y_of(m)) * C + h * 128 + first, 64), count)

    def piece_of(e):
        m = entry(PIECE, e)
        direct = entry(DIRECT, e)
        return m, direct, jnp.where(direct == 1, zl, 1 - zl)

    def send_direct(m):
        rows = code_rows(x, m, zl, 0, 128)
        first = 2 * m - 1 + (m == 0) if isinstance(m, int) else 2 * m - 1
        remote(codes_hbm.at[rows], codes.at[rows], ws, qr.at[first], cross).start()

    def secondary():
        for h in range(2):
            rows = pl.ds(h * 128, 128)
            remote(attn.at[rows], a.at[me, rows], ays, qr.at[32 + h], partner).start()
        for m in range(AHEAD):
            send_direct(m)

        @pl.loop(0, 16 + LAG2)
        def _(n):
            @pl.when(n < 16)
            def _():
                m, direct, h = piece_of(n)
                rows = code_rows(x, m, h, 0, 128)
                wait_all(codes.at[pl.ds(0, 128)], qr.at[n])
                for to in x_nb:
                    remote(codes.at[rows], codes.at[rows], ws, qr.at[16 + n], to).start()

                @pl.when((direct == 1) & (m < 7))
                def _():
                    remote(codes.at[rows], codes.at[rows], ws, qr.at[2 * m + 2], zl_nb).start()

                    @pl.when(m + AHEAD < NY)
                    def _():
                        send_direct(m + AHEAD)

                    @pl.when(m + AHEAD == 7)
                    def _():
                        last = code_rows(x, 7, zl, 0, 128)
                        both = dev(1 - zl, x, 1 - core, zp, y)
                        remote(codes_hbm.at[last], codes.at[last], ws, qr.at[15], both).start()

            @pl.when(n == 1)
            def _():
                @pl.when(zl == 0)
                def _():
                    remote(scales_hbm, scales, scs, scr.at[0], cross).start()

                @pl.when(zl == 1)
                def _():
                    remote(offsets_hbm, offsets, scs, scr.at[1], cross).start()

            @pl.when(n == 6)
            def _():
                @pl.when(zl == 0)
                def _():
                    wait_all(scales, scr.at[0])
                    remote(scales, scales, scs, scr.at[0], zl_nb).start()

                @pl.when(zl == 1)
                def _():
                    wait_all(offsets, scr.at[1])
                    remote(offsets, offsets, scs, scr.at[1], zl_nb).start()

            @pl.when(n == TR_AT)
            def _():
                other = dev(zl, x, core, zr, y)
                remote(plane_cols(zr), tz.at[0, zh], tps, tmr, other).start()
                remote(plane_cols(zq), tz.at[1, zh], tps, tmr, other).start()

            @pl.when(n == TP_AT)
            def _():
                remote(plane_cols(zp), tz.at[0, zh], tps, tpr, partner).start()
                remote(plane_cols(zh), tz.at[1, zh], tps, tpr, partner).start()

            e1 = n - LAG1

            @pl.when((e1 >= 0) & (e1 < 16))
            def _():
                m, direct, h = piece_of(e1)
                wait_all(codes.at[pl.ds(0, 256)], qr.at[16 + e1])
                for d in range(2):
                    q = (x + 3) % 4 if d == 0 else (x + 1) % 4
                    rows = code_rows(q, m, h, d * 64, 64)
                    remote(codes.at[rows], codes.at[rows], ws, qr.at[32 + e1], x_nb[d]).start()

            for r in range(HELLOS):
                @pl.when(n == 2 + 4 * r)
                def _():
                    hear_hello(r)

            m = entry(BLOCK_AT, n)
            s = (m + 1) // 2

            @pl.when(m == 7)
            def _():
                wait_all(t_land.at[0], tcr)
                make_target()

                for i in (0, 1, 3):
                    q = (x + i) % 4
                    wait_all(a.at[0], acr.at[4, index_of(q)])
                    use(q * NY + y_of(7))

            e2 = n - LAG2

            @pl.when(e2 >= 0)
            def _():
                wait_all(codes.at[pl.ds(0, 128)], qr.at[32 + e2])

            @pl.when(m == 7)
            def _():
                q = (x + 2) % 4
                wait_all(a.at[0], acr.at[4, index_of(q)])
                use(q * NY + y_of(7))

            @pl.when((m >= 0) & (m < 7))
            def _():
                @pl.when(m == 0)
                def _():
                    @pl.when(zl == 1)
                    def _():
                        wait_all(scales, scr.at[0])

                    @pl.when(zl == 0)
                    def _():
                        wait_all(offsets, scr.at[1])

                @pl.loop(0, 4)
                def _(k):
                    @pl.when(m == 0)
                    def _():
                        wait_all(a.at[0], acr.at[0, k])

                    @pl.when(m % 2 == 1)
                    def _():
                        wait_all(a.at[pl.ds(0, 2)], acr.at[s, k])

                    use(plane_of(k) * NY + y_of(m))

    say_hello(0)

    @pl.when(prim)
    def _():
        primary()

    @pl.when(sec)
    def _():
        secondary()

    get_lengths.wait()
    total = lengths[0]
    for i in range(1, 32):
        total = total + lengths[i]
    first_seq = 2 * (zl * 8 + x * 2 + prim_core)
    token = lax.broadcasted_iota(jnp.int32, (T, C), 0)
    limit = jnp.where(token < SEQ, lengths[first_seq], lengths[first_seq + 1] + SEQ)
    live = (token < limit).astype(F32)
    cot16 = (2.0 * (acc[...] - target[...]) * live / total.astype(F32)).astype(BF16)
    acc[...] = cot16.astype(F32)

    rs = rowsum[...]
    hi = rs.astype(BF16)
    rest = rs - hi.astype(F32)
    mid = rest.astype(BF16)
    low = (rest - mid.astype(F32)).astype(BF16)
    offs = jnp.dot(hi, cot16, preferred_element_type=F32)
    offs += jnp.dot(mid, cot16, preferred_element_type=F32)
    offs += jnp.dot(low, cot16, preferred_element_type=F32)
    grads[pl.ds(8, 8)] = -offs.reshape(8, 8, C)

    columns_at = jnp.where(prim, zh, zp) * NY + y
    giver = jnp.where(prim, 0, 8) + zl * 4 + x

    def rs_send(c):
        @pl.when(sec | (c != dp))
        def _():
            remote(grads.at[c], rs_land.at[giver], rss, rsr, (c, columns_at)).start()

    def in_order(i):
        return (x + entry([2, 1, 3, 0], i // 2)) % 4 * 2 + (core + 1 + i) % 2

    @pl.loop(0, 8)
    def _(i):
        rs_send(8 + in_order(i))

    @pl.loop(0, 8)
    def _(i):
        c = in_order(i)
        for q in range(8):
            prod = parts[c * 8 + q] * acc[...]
            grads[c, pl.ds(q, 1), :] = jnp.sum(prod, axis=0, keepdims=True)
        rs_send(c)

    @pl.when(prim)
    def _():
        rs_land[giver] = grads[dp]
        wait_all(rs_land.at[pl.ds(0, NDP - 1)], rsr)

    @pl.when(sec)
    def _():
        wait_all(rs_land, rsr)

    out[dp] = jnp.sum(rs_land[...], axis=0)

    for dx in (2, 1, 3, 0):
        for dz in (1, 0):
            for dc in (1, 0):
                if dx + dz + dc > 0:
                    to = dev((zl + dz) % 2, (x + dx) % 4, (core + dc) % 2, zh, y)
                    remote(out.at[dp], out.at[dp], ags, agr, to).start()

    @pl.when(prim)
    def _():
        wait_all(tz.at[0, pl.ds(0, 2)], tps)
        wait_all(a.at[pl.ds(0, 30)], ays)
        wait_all(a, acs)
        wait_all(t_land.at[:, pl.ds(0, NY - 1)], tys)
        wait_all(t_land.at[0], tcs)
        wait_all(rs_land.at[pl.ds(0, NDP - 1)], rss)

    @pl.when(sec)
    def _():
        wait_all(tz.at[0], tps)
        wait_all(a.at[0], ays)
        wait_all(codes, ws)
        wait_all(target.at[pl.ds(0, 128)], scs)
        wait_all(rs_land, rss)

    wait_all(out.at[pl.ds(0, NDP - 1)], ags)
    wait_all(out.at[pl.ds(0, NDP - 1)], agr)


def per_device(attn_out, teacher, int_codes, scales, offsets, lengths, shard_map):
    dma = pltpu.SemaphoreType.DMA
    hbm = pl.BlockSpec(memory_space=pltpu.HBM)
    out = pl.pallas_call(
        kernel,
        out_shape=pltpu.VMEM((NDP, 8, C), F32),
        in_specs=[hbm] * 7,
        out_specs=pl.BlockSpec(memory_space=pltpu.VMEM),
        scratch_shapes=[
            pltpu.SMEM((32,), jnp.int32),
            pltpu.SMEM((32,), jnp.int32),
            pltpu.VMEM((GROUPS, C), F32),
            pltpu.VMEM((GROUPS, C), F32),
            pltpu.VMEM((NT, T, C), BF16),
            pltpu.VMEM((NT * C, C), BF16),
            pltpu.VMEM((GROUPS, T, C), F32),
            pltpu.VMEM((T, C), F32),
            pltpu.VMEM((GROUPS, T), F32),
            pltpu.VMEM((2, NZ, 8, NY * C), BF16),
            pltpu.VMEM((2, NY, NZ, 8, C), BF16),
            pltpu.VMEM((T, C), F32),
            pltpu.VMEM((NDP, 8, C), F32),
            pltpu.VMEM((NDP, 8, C), F32),
            dma((9,)),
            dma(()), dma(()), dma((48,)), dma((5, 4)),
            dma(()), dma(()), dma((2,)),
            dma(()), dma(()), dma(()), dma(()), dma(()), dma(()), dma(()),
            pltpu.SemaphoreType.REGULAR((HELLOS,)),
            dma(()), dma(()), dma(()), dma(()),
        ],
        compiler_params=pltpu.CompilerParams(
            collective_id=0, has_side_effects=True, vmem_limit_bytes=63 << 20
        ),
        cost_estimate=pl.CostEstimate(
            flops=3 * 2 * T * 8192 * C, bytes_accessed=6 << 20, transcendentals=0
        ),
    )(lengths, shard_map, attn_out, teacher, int_codes, scales, offsets)
    flat = out.reshape(128, C)
    return flat[:64], flat[64:]


def solution(mesh):
    in_specs = (
        P("dp", "tensor"),
        P(("dp", "tensor"), None),
        P(None, "tensor"),
        P(None, "tensor"),
        P(None, "tensor"),
        P(),
        P(),
    )
    out_specs = (P(None, "tensor"), P(None, "tensor"))
    return jax.shard_map(
        per_device, mesh=mesh, in_specs=in_specs, out_specs=out_specs, check_vma=False
    )
```

```python
import jax
import jax.numpy as jnp
from jax import lax
from jax.experimental import pallas as pl
from jax.experimental.pallas import tpu as pltpu
from jax.sharding import PartitionSpec as P

SEQ = 128
T = 256
C = 256
NY, NZ = 8, 4
NT = NY * NZ
NDP = 16
GROUPS = 64
F32, BF16 = jnp.float32, jnp.bfloat16
MESH = pl.DeviceIdType.MESH
EVENTS = [
    0, 1, 8, 9, 4, 2, 5, 3, 12, 16, 10, 13, 6, 11, 7, 17, 20, 14, 18, 15,
    21, 19, 22, 24, 25, 23, 28, 26, 29, 27, 30, 32, 33, 31, 36, 34, 37, 35, 38, 39,
]
PIECE = [0, 1, 0, 2, 1, 3, 2, 4, 3, 5, 4, 6, 5, 7, 6, 7]
DIRECT = [1, 1, 0, 1, 0, 1, 0, 1, 0, 1, 0, 1, 0, 1, 0, 0]
LAG1, LAG2 = 4, 8
BLOCK_AT = [-1] * 12 + [0, -1, 1, -1, 2, -1, 3, -1, 4, 5, 6, 7]
AHEAD = 3
TR_AT, TP_AT = 7, 9
TY_AT, TC_AT = 26, 36
HELLOS = 4


def entry(table, n):
    value = jnp.int32(table[0])
    for i, item in enumerate(table):
        value = jnp.where(n == i, item, value)
    return value


def kernel(
    lengths_hbm, shard_map_hbm, attn, teacher, codes_hbm, scales_hbm, offsets_hbm, out,
    lengths, shard_map, scales, offsets, a, codes, parts, acc, rowsum, tz, t_land, target, grads, rs_land,
    loc, ays, acs, qr, acr, ws, scs, scr,
    tps, tpr, tmr, tys, tyr, tcs, tcr, hello, rss, rsr, ags, agr,
):
    dp = lax.axis_index("dp")
    me = lax.axis_index("tensor")
    zh, y = me // NY, me % NY
    zl, x, core = dp // 8, dp // 2 % 4, dp % 2
    prim_core = zh // 2
    prim = core == prim_core
    sec = core != prim_core
    zp = 3 - zh
    zq = zh + 1 - 2 * (zh % 2)
    zr = 3 - zq

    def dev(zl_, x_, core_, zh_, y_):
        return (zl_ * 8 + x_ * 2 + core_, zh_ * NY + y_)

    y_nb = (dev(zl, x, core, zh, (y + 1) % NY), dev(zl, x, core, zh, (y + NY - 1) % NY))
    x_nb = (dev(zl, (x + 1) % 4, core, zh, y), dev(zl, (x + 3) % 4, core, zh, y))
    on_chip = dev(zl, x, 1 - core, zh, y)
    zl_nb = dev(1 - zl, x, core, zh, y)
    mate = dev(zl, x, core, zq, y)
    partner = dev(zl, x, core, zp, y)
    cross = dev(zl, x, 1 - core, zp, y)

    def remote(src, dst, ssem, rsem, to):
        return pltpu.make_async_remote_copy(
            src_ref=src, dst_ref=dst, send_sem=ssem, recv_sem=rsem,
            device_id=to, device_id_type=MESH,
        )

    def wait_all(ref, sem):
        pltpu.make_async_copy(ref, ref, sem).wait()

    near = y_nb + x_nb + (on_chip, zl_nb, mate, partner, cross)
    barrier = pltpu.get_barrier_semaphore()
    for to in near:
        pl.semaphore_signal(barrier, 1, device_id=to, device_id_type=MESH)

    def say_hello(r):
        for to in near:
            pl.semaphore_signal(hello.at[r], 1, device_id=to, device_id_type=MESH)

    def hear_hello(r):
        pl.semaphore_wait(hello.at[r], 9)
        if r + 1 < HELLOS:
            say_hello(r + 1)

    def plane_cols(z):
        return teacher.at[:, pl.ds(pl.multiple_of(z * NY * C, C), NY * C)]

    get_attn = pltpu.make_async_copy(attn, a.at[me], loc.at[0])
    get_codes = pltpu.make_async_copy(codes_hbm, codes, loc.at[1])
    get_scales = pltpu.make_async_copy(scales_hbm, scales, loc.at[2])
    get_offsets = pltpu.make_async_copy(offsets_hbm, offsets, loc.at[3])
    get_lengths = pltpu.make_async_copy(lengths_hbm, lengths, loc.at[4])
    get_map = pltpu.make_async_copy(shard_map_hbm, shard_map, loc.at[5])
    get_t = (
        pltpu.make_async_copy(plane_cols(zh), tz.at[0, zh], loc.at[6]),
        pltpu.make_async_copy(plane_cols(zp), tz.at[1, zh], loc.at[7]),
    )
    own_t = pltpu.make_async_copy(
        tz.at[:, :, :, pl.ds(pl.multiple_of(y * C, C), C)], t_land.at[:, y], loc.at[8]
    )

    @pl.when(prim)
    def _():
        for c in (get_attn, get_codes, get_scales, get_offsets) + get_t:
            c.start()

    get_lengths.start()
    get_map.start()
    acc[...] = jnp.zeros_like(acc)
    rowsum[...] = jnp.zeros_like(rowsum)
    pl.semaphore_wait(barrier, 9)

    group_iota = lax.broadcasted_iota(jnp.int32, (GROUPS, C), 0)
    feat_half = lax.broadcasted_iota(jnp.int32, (GROUPS, C), 1) // 128

    def use(slot):
        block = a[slot]
        halves = []
        for h in range(2):
            rows = pl.ds(pl.multiple_of(slot * C + h * 128, 128), 128)
            g = pl.ds(2 * slot + h, 1)
            piece = codes[rows, :]
            halves.append((piece.astype(F32) * scales[g, :] - offsets[g, :]).astype(BF16))
            parts[2 * slot + h] = jnp.dot(
                block[:, h * 128 : (h + 1) * 128], piece, preferred_element_type=F32
            )
        weight = jnp.concatenate(halves, axis=0)
        acc[...] += jnp.dot(block, weight, preferred_element_type=F32)
        pick = (group_iota == 2 * slot + feat_half).astype(BF16)
        rowsum[...] += lax.dot_general(
            pick, block, (((1,), (1,)), ((), ())), preferred_element_type=F32
        )

    def make_target():
        get_map.wait()
        lane = lax.broadcasted_iota(jnp.int32, (8, T), 1)
        where_to = jnp.zeros((8, T), jnp.int32)
        for j in range(NT):
            where_to = jnp.where(
                lane // 8 == j % NY * NZ + j // NY, shard_map[j] * 8 + lane % 8, where_to
            )
        row = lax.broadcasted_iota(jnp.int32, (T, T), 0)
        perm = (row == where_to[:1, :]).astype(F32).astype(BF16)
        arrived = t_land[0].astype(F32).reshape(T, C).astype(BF16)
        target[...] = jnp.dot(perm, arrived, preferred_element_type=F32)

    def plane_of(k):
        return jnp.where(k == 0, zh, jnp.where(k == 1, zp, jnp.where(k == 2, zq, zr)))

    def index_of(z):
        return jnp.where(z == zh, 0, jnp.where(z == zp, 1, jnp.where(z == zq, 2, 3)))

    def slot_of(s, k, d):
        return plane_of(k) * NY + ((y + NY - s) % NY if d == 0 else (y + s) % NY)

    def half_of(s, kk, d):
        return a.at[slot_of(s, kk // 2, d), pl.ds(pl.multiple_of(kk % 2 * 128, 128), 128)]

    def y_full(s, kk, d):
        ref = half_of(s, kk, d)
        return remote(ref, ref, ays, qr.at[s * 8 + kk], y_nb[d])

    def y_part(kk, d):
        rows = pl.ds(pl.multiple_of(kk % 2 * 128 + d * 64, 64), 64)
        ref = a.at[slot_of(3, kk // 2, d), rows]
        return remote(ref, ref, ays, qr.at[24 + kk], y_nb[d])

    def share(s, k, d):
        ref = a.at[slot_of(s, k, d)]
        return remote(ref, ref, acs, acr.at[s, k], on_chip)

    def ty_copy(i):
        yt = (y + i) % NY
        return remote(
            tz.at[:, :, :, pl.ds(pl.multiple_of(yt * C, C), C)], t_land.at[:, y],
            tys, tyr, dev(zl, x, core, zh, yt),
        )

    def primary():
        get_attn.wait()
        for h in range(2):
            ref = half_of(0, h, 0)
            remote(ref, ref, ays, qr.at[34 + h], mate).start()
            for d in range(2):
                y_full(0, h, d).start()
        share(0, 0, 0).start()
        remote(plane_cols(zq), tz.at[0, zh], tps, tmr, mate).start()
        remote(plane_cols(zr), tz.at[1, zh], tps, tmr, mate).start()
        get_codes.wait()
        get_scales.wait()
        get_offsets.wait()

        @pl.loop(0, len(EVENTS))
        def _(n):
            code = entry(EVENTS, n)
            s, kk = code // 8, code % 8
            k, h = kk // 2, kk % 2

            @pl.when(s == 0)
            def _():
                @pl.when(k > 0)
                def _():
                    wait_all(a.at[0, pl.ds(0, 128)], qr.at[30 + 2 * k + h])

                    @pl.when(k == 1)
                    def _():
                        ref = half_of(0, kk, 0)
                        remote(ref, ref, ays, qr.at[36 + h], mate).start()

                    y_full(0, kk, 0).start()
                    y_full(0, kk, 1).start()

                    @pl.when(h == 1)
                    def _():
                        share(0, k, 0).start()

            @pl.when((s > 0) & (s < 4))
            def _():
                wait_all(a.at[0], qr.at[(s - 1) * 8 + kk])
                for d in range(2):
                    @pl.when(s < 3)
                    def _():
                        y_full(s, kk, d).start()

                    @pl.when(s == 3)
                    def _():
                        y_part(kk, d).start()

                @pl.when(h == 1)
                def _():
                    for d in range(2):
                        share(s, k, d).start()

            @pl.when(s == 4)
            def _():
                wait_all(a.at[0, pl.ds(0, 128)], qr.at[24 + kk])

                @pl.when(h == 1)
                def _():
                    share(4, k, 0).start()

            for r in range(HELLOS):
                @pl.when(n == 4 + 6 * r)
                def _():
                    hear_hello(r)

            @pl.when(n == TY_AT)
            def _():
                for c in get_t:
                    c.wait()
                wait_all(tz.at[0, pl.ds(0, 2)], tpr)
                wait_all(tz.at[0], tmr)
                own_t.start()

                @pl.loop(1, NY)
                def _(i):
                    ty_copy(i).start()

            @pl.when(n == TC_AT)
            def _():
                own_t.wait()
                wait_all(t_land.at[:, pl.ds(0, NY - 1)], tyr)
                remote(t_land.at[1], t_land.at[0], tcs, tcr, on_chip).start()
                make_target()

            @pl.when(h == 1)
            def _():
                use(slot_of(s, k, 0))

            @pl.when((h == 1) & (s > 0) & (s < 4))
            def _():
                use(slot_of(s, k, 1))

    def y_of(m):
        return (y + NY + (m + 1) // 2 * (1 - 2 * (m % 2))) % NY

    def code_rows(q, m, h, first, count):
        return pl.ds(pl.multiple_of((q * NY + y_of(m)) * C + h * 128 + first, 64), count)

    def piece_of(e):
        m = entry(PIECE, e)
        direct = entry(DIRECT, e)
        return m, direct, jnp.where(direct == 1, zl, 1 - zl)

    def send_direct(m):
        rows = code_rows(x, m, zl, 0, 128)
        first = 2 * m - 1 + (m == 0) if isinstance(m, int) else 2 * m - 1
        remote(codes_hbm.at[rows], codes.at[rows], ws, qr.at[first], cross).start()

    def secondary():
        for h in range(2):
            rows = pl.ds(h * 128, 128)
            remote(attn.at[rows], a.at[me, rows], ays, qr.at[32 + h], partner).start()
            send_direct(h)
        for m in range(2, AHEAD):
            send_direct(m)

        @pl.loop(0, 16 + LAG2)
        def _(n):
            @pl.when(n < 16)
            def _():
                m, direct, h = piece_of(n)
                rows = code_rows(x, m, h, 0, 128)
                wait_all(codes.at[pl.ds(0, 128)], qr.at[n])
                for to in x_nb:
                    remote(codes.at[rows], codes.at[rows], ws, qr.at[16 + n], to).start()

                @pl.when((direct == 1) & (m < 7))
                def _():
                    remote(codes.at[rows], codes.at[rows], ws, qr.at[2 * m + 2], zl_nb).start()

                    @pl.when(m + AHEAD < NY)
                    def _():
                        send_direct(m + AHEAD)

                    @pl.when(m + AHEAD == 7)
                    def _():
                        last = code_rows(x, 7, zl, 0, 128)
                        both = dev(1 - zl, x, 1 - core, zp, y)
                        remote(codes_hbm.at[last], codes.at[last], ws, qr.at[15], both).start()

            @pl.when(n == 1)
            def _():
                @pl.when(zl == 0)
                def _():
                    remote(scales_hbm, scales, scs, scr.at[0], cross).start()

                @pl.when(zl == 1)
                def _():
                    remote(offsets_hbm, offsets, scs, scr.at[1], cross).start()

            @pl.when(n == 6)
            def _():
                @pl.when(zl == 0)
                def _():
                    wait_all(scales, scr.at[0])
                    remote(scales, scales, scs, scr.at[0], zl_nb).start()

                @pl.when(zl == 1)
                def _():
                    wait_all(offsets, scr.at[1])
                    remote(offsets, offsets, scs, scr.at[1], zl_nb).start()

            @pl.when(n == TR_AT)
            def _():
                other = dev(zl, x, core, zr, y)
                remote(plane_cols(zr), tz.at[0, zh], tps, tmr, other).start()
                remote(plane_cols(zq), tz.at[1, zh], tps, tmr, other).start()

            @pl.when(n == TP_AT)
            def _():
                remote(plane_cols(zp), tz.at[0, zh], tps, tpr, partner).start()
                remote(plane_cols(zh), tz.at[1, zh], tps, tpr, partner).start()

            e1 = n - LAG1

            @pl.when((e1 >= 0) & (e1 < 16))
            def _():
                m, direct, h = piece_of(e1)
                wait_all(codes.at[pl.ds(0, 256)], qr.at[16 + e1])
                for d in range(2):
                    q = (x + 3) % 4 if d == 0 else (x + 1) % 4
                    rows = code_rows(q, m, h, d * 64, 64)
                    remote(codes.at[rows], codes.at[rows], ws, qr.at[32 + e1], x_nb[d]).start()

            for r in range(HELLOS):
                @pl.when(n == 2 + 4 * r)
                def _():
                    hear_hello(r)

            m = entry(BLOCK_AT, n)
            s = (m + 1) // 2

            @pl.when(m == 7)
            def _():
                wait_all(t_land.at[0], tcr)
                make_target()

                for i in (0, 1, 3):
                    q = (x + i) % 4
                    wait_all(a.at[0], acr.at[4, index_of(q)])
                    use(q * NY + y_of(7))

            e2 = n - LAG2

            @pl.when(e2 >= 0)
            def _():
                wait_all(codes.at[pl.ds(0, 128)], qr.at[32 + e2])

            @pl.when(m == 7)
            def _():
                q = (x + 2) % 4
                wait_all(a.at[0], acr.at[4, index_of(q)])
                use(q * NY + y_of(7))

            @pl.when((m >= 0) & (m < 7))
            def _():
                @pl.when(m == 0)
                def _():
                    @pl.when(zl == 1)
                    def _():
                        wait_all(scales, scr.at[0])

                    @pl.when(zl == 0)
                    def _():
                        wait_all(offsets, scr.at[1])

                @pl.loop(0, 4)
                def _(k):
                    @pl.when(m == 0)
                    def _():
                        wait_all(a.at[0], acr.at[0, k])

                    @pl.when(m % 2 == 1)
                    def _():
                        wait_all(a.at[pl.ds(0, 2)], acr.at[s, k])

                    use(plane_of(k) * NY + y_of(m))

    say_hello(0)

    @pl.when(prim)
    def _():
        primary()

    @pl.when(sec)
    def _():
        secondary()

    get_lengths.wait()
    total = lengths[0]
    for i in range(1, 32):
        total = total + lengths[i]
    first_seq = 2 * (zl * 8 + x * 2 + prim_core)
    token = lax.broadcasted_iota(jnp.int32, (T, C), 0)
    limit = jnp.where(token < SEQ, lengths[first_seq], lengths[first_seq + 1] + SEQ)
    live = (token < limit).astype(F32)
    cot16 = (2.0 * (acc[...] - target[...]) * live / total.astype(F32)).astype(BF16)
    acc[...] = cot16.astype(F32)

    rs = rowsum[...]
    hi = rs.astype(BF16)
    rest = rs - hi.astype(F32)
    mid = rest.astype(BF16)
    low = (rest - mid.astype(F32)).astype(BF16)
    offs = jnp.dot(hi, cot16, preferred_element_type=F32)
    offs += jnp.dot(mid, cot16, preferred_element_type=F32)
    offs += jnp.dot(low, cot16, preferred_element_type=F32)
    grads[pl.ds(8, 8)] = -offs.reshape(8, 8, C)

    columns_at = jnp.where(prim, zh, zp) * NY + y
    giver = jnp.where(prim, 0, 8) + zl * 4 + x

    def rs_send(c):
        @pl.when(sec | (c != dp))
        def _():
            remote(grads.at[c], rs_land.at[giver], rss, rsr, (c, columns_at)).start()

    def in_order(i):
        return (x + entry([2, 1, 3, 0], i // 2)) % 4 * 2 + (core + 1 + i) % 2

    @pl.loop(0, 8)
    def _(i):
        rs_send(8 + in_order(i))

    @pl.loop(0, 8)
    def _(i):
        c = in_order(i)
        for q in range(8):
            prod = parts[c * 8 + q] * acc[...]
            grads[c, pl.ds(q, 1), :] = jnp.sum(prod, axis=0, keepdims=True)
        rs_send(c)

    @pl.when(prim)
    def _():
        rs_land[giver] = grads[dp]
        wait_all(rs_land.at[pl.ds(0, NDP - 1)], rsr)

    @pl.when(sec)
    def _():
        wait_all(rs_land, rsr)

    out[dp] = jnp.sum(rs_land[...], axis=0)

    for dx in (2, 1, 3, 0):
        for dz in (1, 0):
            for dc in (1, 0):
                if dx + dz + dc > 0:
                    to = dev((zl + dz) % 2, (x + dx) % 4, (core + dc) % 2, zh, y)
                    remote(out.at[dp], out.at[dp], ags, agr, to).start()

    @pl.when(prim)
    def _():
        wait_all(tz.at[0, pl.ds(0, 2)], tps)
        wait_all(a.at[pl.ds(0, 30)], ays)
        wait_all(a, acs)
        wait_all(t_land.at[:, pl.ds(0, NY - 1)], tys)
        wait_all(t_land.at[0], tcs)
        wait_all(rs_land.at[pl.ds(0, NDP - 1)], rss)

    @pl.when(sec)
    def _():
        wait_all(tz.at[0], tps)
        wait_all(a.at[0], ays)
        wait_all(codes, ws)
        wait_all(target.at[pl.ds(0, 128)], scs)
        wait_all(rs_land, rss)

    wait_all(out.at[pl.ds(0, NDP - 1)], ags)
    wait_all(out.at[pl.ds(0, NDP - 1)], agr)


def per_device(attn_out, teacher, int_codes, scales, offsets, lengths, shard_map):
    dma = pltpu.SemaphoreType.DMA
    hbm = pl.BlockSpec(memory_space=pltpu.HBM)
    out = pl.pallas_call(
        kernel,
        out_shape=pltpu.VMEM((NDP, 8, C), F32),
        in_specs=[hbm] * 7,
        out_specs=pl.BlockSpec(memory_space=pltpu.VMEM),
        scratch_shapes=[
            pltpu.SMEM((32,), jnp.int32),
            pltpu.SMEM((32,), jnp.int32),
            pltpu.VMEM((GROUPS, C), F32),
            pltpu.VMEM((GROUPS, C), F32),
            pltpu.VMEM((NT, T, C), BF16),
            pltpu.VMEM((NT * C, C), BF16),
            pltpu.VMEM((GROUPS, T, C), F32),
            pltpu.VMEM((T, C), F32),
            pltpu.VMEM((GROUPS, T), F32),
            pltpu.VMEM((2, NZ, 8, NY * C), BF16),
            pltpu.VMEM((2, NY, NZ, 8, C), BF16),
            pltpu.VMEM((T, C), F32),
            pltpu.VMEM((NDP, 8, C), F32),
            pltpu.VMEM((NDP, 8, C), F32),
            dma((9,)),
            dma(()), dma(()), dma((48,)), dma((5, 4)),
            dma(()), dma(()), dma((2,)),
            dma(()), dma(()), dma(()), dma(()), dma(()), dma(()), dma(()),
            pltpu.SemaphoreType.REGULAR((HELLOS,)),
            dma(()), dma(()), dma(()), dma(()),
        ],
        compiler_params=pltpu.CompilerParams(
            collective_id=0, has_side_effects=True, vmem_limit_bytes=63 << 20
        ),
        cost_estimate=pl.CostEstimate(
            flops=3 * 2 * T * 8192 * C, bytes_accessed=6 << 20, transcendentals=0
        ),
    )(lengths, shard_map, attn_out, teacher, int_codes, scales, offsets)
    flat = out.reshape(128, C)
    return flat[:64], flat[64:]


def solution(mesh):
    in_specs = (
        P("dp", "tensor"),
        P(("dp", "tensor"), None),
        P(None, "tensor"),
        P(None, "tensor"),
        P(None, "tensor"),
        P(),
        P(),
    )
    out_specs = (P(None, "tensor"), P(None, "tensor"))
    return jax.shard_map(
        per_device, mesh=mesh, in_specs=in_specs, out_specs=out_specs, check_vma=False
    )
```
